32 devices in a mesh: pipe: 4 (over z), dp: 8 (over y, x, core).
Axes of the slice: x: 2, y: 2, z: 4, core: 2. Of those that a mesh axis runs over, the one named last changes fastest.
Arguments:
- acts_in: bfloat16 [2, 512, 4096], P(None, 'dp'), may hold values from -40 to 40
- cotangent: bfloat16 [2, 512, 4096], P(None, 'dp'), may hold values from -6 to 6
- norm_gains: float32 [4, 4096], P('pipe'), may hold values from 0.1 to 1.9
- weights: bfloat16 [4, 256, 128, 128], P('pipe', 'dp'), may hold values from -0.1875 to 0.1875
- tile_columns: int32 [4, 256], P('pipe'), may hold values from 0 to 31, as said below
- lengths: int32 [2, 8], P(None, 'dp'), may hold values from 16 to 64
Outputs:
- section_out: bfloat16 [4, 2, 512, 4096], P('pipe', None, 'dp')
- input_grad: bfloat16 [4, 2, 512, 4096], P('pipe', None, 'dp')
- weight_grad: float32 [4, 256, 128, 128], P('pipe', 'dp')
The draws below stay inside these ranges and needn't reach their ends.
Inputs may be any that keep to these rules, and one draw needn't show every extreme that they name: `tile_columns`: the 8 entries of one block row of a section (positions r * 8 to r * 8 + 7) are distinct.
All inputs are finite; a program needn't handle non-finite values.
Results may differ from the reference program's by a relative error of at most 0.0081.
Values may be sent and summed in bfloat16 or wider, within the bound.
A program may use at most 384 MiB of HBM per device.

```python
import math
import jax
import jax.numpy as jnp
from jax import lax

D = 4096
TILE = 128
KEEP = 8
M = 2
BLOCKS = 32
TILES = 256
TOKENS = 512
LENGTH = 64
SEQS = 8
N_PIPE = 4


def draw_acts_in(key, part):
    shape_all = (M, TOKENS, D)
    keys = jax.random.split(key, 3)
    base = jax.random.truncated_normal(keys[0], -6.0, 6.0, shape_all, jnp.float32)
    row_scale = jnp.exp(jax.random.uniform(keys[1], (M, TOKENS, 1), jnp.float32, math.log(0.3), math.log(3.0)))
    column_scale = jnp.exp(jax.random.uniform(keys[2], (1, 1, D), jnp.float32, math.log(0.3), math.log(3.0)))
    return jnp.clip(base * row_scale * column_scale, -40.0, 40.0).astype(jnp.bfloat16)


def draw_tile_columns(key, part):
    row_keys = jax.random.split(jax.random.fold_in(key, 11), N_PIPE * BLOCKS)
    orders = jax.vmap(lambda row_key: jax.random.permutation(row_key, BLOCKS))(row_keys)
    return orders[:, :KEEP].reshape(N_PIPE, BLOCKS * KEEP).astype(jnp.int32)


def plant(result, own_key, least, high):
    longest = result.shape.index(max(result.shape))
    spots = []
    for shift in (0, 1):
        where = [jax.random.randint(jax.random.fold_in(own_key, axis), (), 0, length) for axis, length in enumerate(result.shape)]
        where[longest] = (where[longest] + shift) % result.shape[longest]
        spots.append(tuple(where))
    return result.at[spots[0]].set(least).at[spots[1]].set(high)


def block_scale(key, extent, shards, low, top_value):
    factor_of, own = 1.0, jax.random.fold_in(key, 6)
    for axis_at, parts in shards:
        steps = jnp.exp(jax.random.uniform(jax.random.fold_in(own, axis_at), (parts,), jnp.float32, low / len(shards), top_value / len(shards)))
        factor_of = factor_of * jnp.repeat(steps, extent[axis_at] // parts).reshape([-1 if axis == axis_at else 1 for axis in range(len(extent))])
    return factor_of


def normal_values(key, shape, deviation, limit, shards=(), held_as=jnp.bfloat16):
    array = deviation * jax.random.normal(key, shape, jnp.float32)
    if shards:
        array = array * block_scale(key, shape, shards, -0.22, 0.18)
    return jnp.clip(array, -limit, limit).astype(held_as)


def setup_inputs(seed: int = 0) -> dict:
    key_of = jax.random.split(jax.random.key(seed), 7)
    acts_in = draw_acts_in(jax.random.fold_in(key_of[6], 71), 0)
    cotangent = normal_values(key_of[1], (M, TOKENS, D), 1.0, 6.0, ((1, 8),))
    norm_gains = jnp.clip(1.0 + 0.18 * jax.random.normal(key_of[2], (N_PIPE, D), jnp.float32), 0.1, 1.9)
    weights = normal_values(key_of[3], (N_PIPE, TILES, TILE, TILE), (KEEP * TILE) ** -0.5, 0.1875, ((0, 4), (1, 8)))
    tile_columns = draw_tile_columns(jax.random.fold_in(key_of[6], 71), 0)
    lengths = plant(jax.random.randint(key_of[5], (M, SEQS), LENGTH // 4, LENGTH + 1), jax.random.fold_in(key_of[5], 1), LENGTH // 4, LENGTH).astype(jnp.int32)
    return {"acts_in": acts_in, "cotangent": cotangent, "norm_gains": norm_gains, "weights": weights, "tile_columns": tile_columns, "lengths": lengths}


epsilon = 1e-05

def row_mask(length_row):
    position = jnp.arange(TOKENS, dtype=jnp.int32)
    sequence = position // LENGTH
    within = position - sequence * LENGTH
    match_table = sequence[:, None] == jnp.arange(SEQS, dtype=jnp.int32)[None, :]
    length_limit = lax.optimization_barrier(jnp.sum(jnp.where(match_table, length_row[None, :], 0), axis=1))
    return (within < length_limit).astype(jnp.float32)

def normalize(section_input, section_gain):
    values = section_input.astype(jnp.float32)
    inv_rms = lax.rsqrt(lax.optimization_barrier(jnp.mean(values * values, axis=-1, keepdims=True)) + epsilon)
    unit_rows = values * inv_rms
    return (values, inv_rms, unit_rows, (unit_rows * section_gain).astype(jnp.bfloat16))

def block_rows_of(hidden):
    return jnp.transpose(hidden.astype(jnp.float32).reshape(TOKENS, BLOCKS, TILE), (1, 0, 2))

def sparse_forward(hidden, tile_grid, column_table):

    def add_block(total_sum, pieces):
        block_rows, block_tiles, block_columns = pieces
        contrib = jnp.einsum('tk,jkn->tjn', block_rows, block_tiles.astype(jnp.float32), precision=lax.Precision.HIGHEST)
        return (total_sum.at[:, block_columns, :].add(contrib), None)
    start_sum = jnp.zeros((TOKENS, BLOCKS, TILE), jnp.float32)
    total_sum, unused = lax.scan(add_block, start_sum, (block_rows_of(hidden), tile_grid, column_table))
    return total_sum.reshape(TOKENS, D)

def sparse_backward(hidden, pre_delta, tile_grid, column_table):
    delta_blocks = pre_delta.astype(jnp.float32).reshape(TOKENS, BLOCKS, TILE)

    def one_block(carried, pieces):
        block_rows, block_tiles, block_columns = pieces
        picked = jnp.take(delta_blocks, block_columns, axis=1)
        tile_grad = jnp.einsum('tk,tjn->jkn', block_rows, picked, precision=lax.Precision.HIGHEST)
        row_delta = jnp.einsum('tjn,jkn->tk', picked, block_tiles.astype(jnp.float32), precision=lax.Precision.HIGHEST)
        return (carried, (tile_grad, row_delta))
    carried, outcome = lax.scan(one_block, jnp.zeros((), jnp.float32), (block_rows_of(hidden), tile_grid, column_table))
    tile_grads, row_deltas = outcome
    return (tile_grads.reshape(TILES, TILE, TILE), jnp.transpose(row_deltas, (1, 0, 2)).reshape(TOKENS, D))

def reference(acts_in, cotangent, norm_gains, weights, tile_columns, lengths):
    grids = weights.reshape(N_PIPE, BLOCKS, KEEP, TILE, TILE)
    tables = tile_columns.reshape(N_PIPE, BLOCKS, KEEP).astype(jnp.int32)
    outputs = [[None] * M for section_id in range(N_PIPE)]
    grads = [[None] * M for section_id in range(N_PIPE)]
    saved = [[None] * M for section_id in range(N_PIPE)]
    for micro_id in range(M):
        section_input = acts_in[micro_id]
        for section_id in range(N_PIPE):
            values, inv_rms, unit_rows, hidden = normalize(section_input, norm_gains[section_id])
            pre_act = sparse_forward(hidden, grids[section_id], tables[section_id])
            section_result = (values + jax.nn.silu(pre_act)).astype(jnp.bfloat16)
            saved[section_id][micro_id] = (section_input, pre_act)
            outputs[section_id][micro_id] = section_result
            section_input = section_result
    tile_sums = [jnp.zeros((TILES, TILE, TILE), jnp.float32) for section_id in range(N_PIPE)]
    for micro_id in range(M):
        grad_input = (cotangent[micro_id].astype(jnp.float32) * row_mask(lengths[micro_id])[:, None]).astype(jnp.bfloat16)
        for section_id in reversed(range(N_PIPE)):
            section_input, pre_act = saved[section_id][micro_id]
            values, inv_rms, unit_rows, hidden = normalize(section_input, norm_gains[section_id])
            sigmoid_part = jax.nn.sigmoid(pre_act)
            grad_float = grad_input.astype(jnp.float32)
            pre_delta = (grad_float * sigmoid_part * (1.0 + pre_act * (1.0 - sigmoid_part))).astype(jnp.bfloat16)
            tile_grad, hidden_delta = sparse_backward(hidden, pre_delta, grids[section_id], tables[section_id])
            tile_sums[section_id] = tile_sums[section_id] + tile_grad
            gained = hidden_delta * norm_gains[section_id]
            input_delta = grad_float + inv_rms * (gained - unit_rows * lax.optimization_barrier(jnp.mean(gained * unit_rows, axis=-1, keepdims=True)))
            grad_input = input_delta.astype(jnp.bfloat16)
            grads[section_id][micro_id] = grad_input
    section_out = jnp.stack([jnp.stack(outputs[section_id]) for section_id in range(N_PIPE)])
    input_grad = jnp.stack([jnp.stack(grads[section_id]) for section_id in range(N_PIPE)])
    return (section_out, input_grad, jnp.stack(tile_sums))
```

```python
import functools

import jax
import jax.numpy as jnp
from jax import lax
from jax.experimental import pallas as pl
from jax.experimental.pallas import tpu as pltpu
from jax.sharding import PartitionSpec as P

KEEP = 8
EPSILON = 1e-05
ROWS_PER_STEP = 4
VMEM_BYTES = 48 * 1024 * 1024

F32 = jnp.float32
BF16 = jnp.bfloat16


def sigmoid(v):
    return 1.0 / (1.0 + jnp.exp(-v))


def columns(block, tile):
    return pl.ds(block * tile, tile)


def forward_kernel(state, cols, acts, received, gain, tiles, *refs):
    y_ref, out_ref, x_ref, pre_ref, hid_ref = refs[-5:]
    blocks, _, tile = pre_ref.shape[1:]
    step = pl.program_id(0)
    live = state[0] > 0
    first = state[2] > 0

    @pl.when(jnp.logical_and(live, step == 0))
    def _():
        @pl.when(first)
        def _():
            x_ref[0] = acts[0]

        @pl.when(jnp.logical_not(first))
        def _():
            x_ref[0] = received[...]

        total = jnp.zeros(pre_ref.shape[2:], F32)
        for r in range(blocks):
            v = x_ref[0, :, columns(r, tile)].astype(F32)
            total = total + v * v
        mean = jnp.sum(total, axis=1, keepdims=True) * (1.0 / (blocks * tile))
        inv_rms = lax.rsqrt(mean + EPSILON)
        for r in range(blocks):
            v = x_ref[0, :, columns(r, tile)].astype(F32)
            hid_ref[0, r] = ((v * inv_rms) * gain[:, columns(r, tile)]).astype(BF16)
        pre_ref[...] = jnp.zeros_like(pre_ref)

    @pl.when(live)
    def _():
        for i in range(ROWS_PER_STEP):
            r = step * ROWS_PER_STEP + i
            wide = jnp.concatenate([tiles[i * KEEP + j] for j in range(KEEP)], axis=1)
            parts = jnp.dot(hid_ref[0, r], wide, preferred_element_type=F32)
            for j in range(KEEP):
                c = cols[r * KEEP + j]
                pre_ref[0, c] += parts[:, j * tile : (j + 1) * tile]

    @pl.when(jnp.logical_and(live, step == pl.num_programs(0) - 1))
    def _():
        for r in range(blocks):
            v = x_ref[0, :, columns(r, tile)].astype(F32)
            p = pre_ref[0, r]
            y = (v + p * sigmoid(p)).astype(BF16)
            y_ref[:, columns(r, tile)] = y
            out_ref[0, :, columns(r, tile)] = y


def slot_block(shape):
    return pl.BlockSpec((1, *shape), lambda s, state, cols: (state[1],) + (0,) * len(shape))


def whole_block(shape):
    return pl.BlockSpec(shape, lambda s, state, cols: (0,) * len(shape))


def micro_block(shape):
    return pl.BlockSpec((1, *shape), lambda s, state, cols: (state[3],) + (0,) * len(shape))


def tile_block(tile):
    return pl.BlockSpec(
        (ROWS_PER_STEP * KEEP, tile, tile), lambda s, state, cols: (s, 0, 0)
    )


def run_forward(state, cols, acts, received, gain, gathered, kept):
    micros, rows, width = acts.shape
    tile = gathered.shape[1]
    blocks = width // tile
    flat, cut = (rows, width), (blocks, rows, tile)
    old = [] if kept is None else list(kept)
    return pl.pallas_call(
        forward_kernel,
        grid_spec=pltpu.PrefetchScalarGridSpec(
            num_scalar_prefetch=2,
            grid=(blocks // ROWS_PER_STEP,),
            in_specs=[
                micro_block(flat),
                whole_block(flat),
                whole_block((1, width)),
                tile_block(tile),
            ]
            + [pl.BlockSpec(memory_space=pl.ANY)] * len(old),
            out_specs=[
                whole_block(flat),
                slot_block(flat),
                slot_block(flat),
                slot_block(cut),
                slot_block(cut),
            ],
        ),
        out_shape=[
            jax.ShapeDtypeStruct(flat, BF16),
            jax.ShapeDtypeStruct((micros + 1, *flat), BF16),
            jax.ShapeDtypeStruct((micros + 1, *flat), BF16),
            jax.ShapeDtypeStruct((micros + 1, *cut), F32),
            jax.ShapeDtypeStruct((micros + 1, *cut), BF16),
        ],
        input_output_aliases={6 + i: 1 + i for i in range(len(old))},
        compiler_params=pltpu.CompilerParams(vmem_limit_bytes=VMEM_BYTES),
        cost_estimate=pl.CostEstimate(
            flops=2 * rows * KEEP * width * tile,
            bytes_accessed=gathered.size * 2,
            transcendentals=rows * width,
        ),
        name="section_forward",
    )(state, cols, acts, received, gain, gathered, *old)


def backward_kernel(state, cols, cot, received, gain, tiles, x_in, pre_in, *refs):
    g_ref, grad_ref, pd_ref, gained_ref, g_all, inv_ref, dot_ref = refs[-7:]
    blocks, rows, tile = pre_in.shape[1:]
    step = pl.program_id(0)
    live = state[0] > 0
    last = state[2] > 0

    @pl.when(jnp.logical_and(live, step == 0))
    def _():
        @pl.when(last)
        def _():
            place = lax.broadcasted_iota(jnp.int32, (rows, tile), 0)
            valid = (place < state[4]).astype(F32)
            for r in range(blocks):
                g_all[r] = (cot[0, :, columns(r, tile)].astype(F32) * valid).astype(BF16)

        @pl.when(jnp.logical_not(last))
        def _():
            for r in range(blocks):
                g_all[r] = received[:, columns(r, tile)]

        total = jnp.zeros((rows, tile), F32)
        for r in range(blocks):
            p = pre_in[0, r]
            s = sigmoid(p)
            g = g_all[r].astype(F32)
            pd_ref[0, r] = (g * s * (1.0 + p * (1.0 - s))).astype(BF16)
            v = x_in[0, :, columns(r, tile)].astype(F32)
            total = total + v * v
        mean = jnp.sum(total, axis=1, keepdims=True) * (1.0 / (blocks * tile))
        inv_ref[...] = jnp.broadcast_to(lax.rsqrt(mean + EPSILON), inv_ref.shape)
        dot_ref[...] = jnp.zeros_like(dot_ref)

    @pl.when(live)
    def _():
        for i in range(ROWS_PER_STEP):
            r = step * ROWS_PER_STEP + i
            wide = jnp.concatenate([tiles[i * KEEP + j] for j in range(KEEP)], axis=1)
            picked = jnp.concatenate(
                [pd_ref[0, cols[r * KEEP + j]] for j in range(KEEP)], axis=1
            )
            delta = lax.dot_general(
                picked, wide, (((1,), (1,)), ((), ())), preferred_element_type=F32
            )
            here = pl.ds(pl.multiple_of(r * tile, tile), tile)
            gained = delta * gain[:, here]
            gained_ref[r] = gained
            unit = x_in[0, :, here].astype(F32) * inv_ref[...]
            dot_ref[...] += gained * unit

    @pl.when(jnp.logical_and(live, step == pl.num_programs(0) - 1))
    def _():
        mean = jnp.sum(dot_ref[...], axis=1, keepdims=True) * (1.0 / (blocks * tile))
        inv = inv_ref[...]
        for r in range(blocks):
            unit = x_in[0, :, columns(r, tile)].astype(F32) * inv
            g = g_all[r].astype(F32) + inv * (gained_ref[r] - unit * mean)
            g = g.astype(BF16)
            g_ref[:, columns(r, tile)] = g
            grad_ref[0, :, columns(r, tile)] = g


def run_backward(state, cols, cot, received, gain, gathered, x_all, pre_all, kept):
    micros, rows, width = cot.shape
    tile = gathered.shape[1]
    blocks = width // tile
    flat, cut = (rows, width), (blocks, rows, tile)
    old = [] if kept is None else list(kept)
    return pl.pallas_call(
        backward_kernel,
        grid_spec=pltpu.PrefetchScalarGridSpec(
            num_scalar_prefetch=2,
            grid=(blocks // ROWS_PER_STEP,),
            in_specs=[
                micro_block(flat),
                whole_block(flat),
                whole_block((1, width)),
                tile_block(tile),
                slot_block(flat),
                slot_block(cut),
            ]
            + [pl.BlockSpec(memory_space=pl.ANY)] * len(old),
            out_specs=[whole_block(flat), slot_block(flat), slot_block(cut)],
            scratch_shapes=[
                pltpu.VMEM(cut, F32),
                pltpu.VMEM(cut, BF16),
                pltpu.VMEM((rows, tile), F32),
                pltpu.VMEM((rows, tile), F32),
            ],
        ),
        out_shape=[
            jax.ShapeDtypeStruct(flat, BF16),
            jax.ShapeDtypeStruct((micros + 1, *flat), BF16),
            jax.ShapeDtypeStruct((micros + 1, *cut), BF16),
        ],
        input_output_aliases={8 + i: 1 + i for i in range(len(old))},
        compiler_params=pltpu.CompilerParams(vmem_limit_bytes=VMEM_BYTES),
        cost_estimate=pl.CostEstimate(
            flops=2 * rows * KEEP * width * tile,
            bytes_accessed=gathered.size * 2,
            transcendentals=rows * width,
        ),
        name="section_backward",
    )(state, cols, cot, received, gain, gathered, x_all, pre_all, *old)


def tile_grad_kernel(per_group, micros, base, cols, hidden, *refs):
    deltas, out_ref = refs[:micros], refs[micros]
    share, _, _, rows, tile = hidden.shape
    start = base[0] + pl.program_id(0) * per_group
    total = None
    for m in range(micros):
        left = hidden[:, m, 0].reshape(share * rows, tile)
        right = jnp.concatenate(
            [
                deltas[m][:, cols[start + j]].reshape(share * rows, tile)
                for j in range(per_group)
            ],
            axis=1,
        )
        term = lax.dot_general(
            left, right, (((0,), (0,)), ((), ())), preferred_element_type=F32
        )
        total = term if total is None else total + term

    @pl.when(pl.program_id(1) == 0)
    def _():
        for j in range(per_group):
            out_ref[j] = total[:, j * tile : (j + 1) * tile]

    @pl.when(pl.program_id(1) > 0)
    def _():
        for j in range(per_group):
            out_ref[j] += total[:, j * tile : (j + 1) * tile]


def run_tile_grad(base, cols, hidden, deltas, tile_count):
    devices, micros, blocks, rows, tile = hidden.shape
    per_group = min(tile_count, KEEP)
    share = min(devices, 8)
    return pl.pallas_call(
        functools.partial(tile_grad_kernel, per_group, micros),
        grid_spec=pltpu.PrefetchScalarGridSpec(
            num_scalar_prefetch=2,
            grid=(tile_count // per_group, devices // share),
            in_specs=[
                pl.BlockSpec(
                    (share, micros, 1, rows, tile),
                    lambda i, k, base, cols: (k, 0, (base[0] + i * per_group) // KEEP, 0, 0),
                )
            ]
            + [
                pl.BlockSpec(
                    (share, blocks, rows, tile), lambda i, k, base, cols: (k, 0, 0, 0)
                )
            ]
            * micros,
            out_specs=pl.BlockSpec(
                (per_group, tile, tile), lambda i, k, base, cols: (i, 0, 0)
            ),
        ),
        out_shape=jax.ShapeDtypeStruct((tile_count, tile, tile), F32),
        compiler_params=pltpu.CompilerParams(vmem_limit_bytes=VMEM_BYTES),
        cost_estimate=pl.CostEstimate(
            flops=2 * tile_count * tile * tile * devices * rows * micros,
            bytes_accessed=2 * devices * micros * blocks * rows * tile,
            transcendentals=0,
        ),
        name="tile_grad",
    )(base, cols, hidden, *deltas)


def relay(value, steps):
    count = lax.axis_size("pipe")
    low, high = max(0, -steps), min(count, count - steps)
    return lax.ppermute(value, "pipe", [(i, i + steps) for i in range(low, high)])


def on_device(acts_in, cotangent, norm_gains, weights, tile_columns, lengths):
    micros, rows, width = acts_in.shape
    sections = lax.axis_size("pipe")
    here = lax.axis_index("pipe")
    cols = tile_columns[0]
    tile_count = weights.shape[1]
    gathered = lax.all_gather(weights[0], "dp", axis=0, tiled=True)
    ticks = micros + sections - 1

    def state_of(micro, special):
        live = jnp.logical_and(micro >= 0, micro < micros)
        near = jnp.clip(micro, 0, micros - 1)
        slot = jnp.where(live, near, micros)
        length = lax.dynamic_index_in_dim(lengths[:, 0], near, 0, keepdims=False)
        return jnp.stack([live.astype(jnp.int32), slot, special.astype(jnp.int32), near, length])

    received = acts_in[0]
    kept = None
    for tick in range(ticks):
        state = state_of(tick - here, here == 0)
        y, *kept = run_forward(state, cols, acts_in, received, norm_gains, gathered, kept)
        if tick < ticks - 1:
            received = relay(y, 1)
    section_out, x_all, pre_all, hid_all = kept
    hidden = lax.all_gather(hid_all[:micros], "dp", axis=0)

    received = acts_in[0]
    kept = None
    deltas = []
    for tick in range(ticks):
        state = state_of(tick - (sections - 1 - here), here == sections - 1)
        g, *kept = run_backward(
            state, cols, cotangent, received, norm_gains, gathered, x_all, pre_all, kept
        )
        if tick >= sections - 1:
            deltas.append(lax.all_gather(kept[1][tick - sections + 1], "dp", axis=0))
        if tick < ticks - 1:
            received = relay(g, -1)
    input_grad = kept[0]
    base = (lax.axis_index("dp") * tile_count).astype(jnp.int32).reshape(1)
    weight_grad = run_tile_grad(base, cols, hidden, deltas, tile_count)
    return (section_out[:micros][None], input_grad[:micros][None], weight_grad[None])


def solution(mesh):
    return jax.shard_map(
        on_device,
        mesh=mesh,
        in_specs=(
            P(None, "dp", None),
            P(None, "dp", None),
            P("pipe", None),
            P("pipe", "dp", None, None),
            P("pipe", None),
            P(None, "dp"),
        ),
        out_specs=(
            P("pipe", None, "dp", None),
            P("pipe", None, "dp", None),
            P("pipe", "dp", None, None),
        ),
        check_vma=False,
    )
```

```python
import functools

import jax
import jax.numpy as jnp
from jax import lax
from jax.experimental import pallas as pl
from jax.experimental.pallas import tpu as pltpu
from jax.sharding import PartitionSpec as P

KEEP = 8
EPSILON = 1e-05
ROWS_PER_STEP = 4
SPLIT = 2
VMEM_BYTES = 48 * 1024 * 1024

F32 = jnp.float32
BF16 = jnp.bfloat16


def sigmoid(v):
    return 1.0 / (1.0 + jnp.exp(-v))


def columns(block, tile):
    return pl.ds(block * tile, tile)


def greet():
    here, count = lax.axis_index("pipe"), lax.axis_size("pipe")
    barrier = pltpu.get_barrier_semaphore()
    for other in (lax.rem(here + 1, count), lax.rem(here + count - 1, count)):
        pl.semaphore_signal(
            barrier, inc=1, device_id={"pipe": other}, device_id_type=pl.DeviceIdType.MESH
        )
    pl.semaphore_wait(barrier, 2)


def hop(source, landing, send_sems, recv_sems, chunk, target):
    return pltpu.make_async_remote_copy(
        src_ref=source.at[chunk],
        dst_ref=landing.at[chunk],
        send_sem=send_sems.at[chunk],
        recv_sem=recv_sems.at[chunk],
        device_id={"pipe": target},
        device_id_type=pl.DeviceIdType.MESH,
    )


def forward_kernel(
    order, keep, last_of, filled, acts, gain, tiles,
    out_ref, x_ref, pre_ref, hid_ref,
    landing, parts_ref, sums_ref, send_sems, recv_sems,
):
    chunks, blocks, rows, tile = pre_ref.shape
    here, count = lax.axis_index("pipe"), lax.axis_size("pipe")
    target = lax.rem(here + 1, count)
    greet()

    def one_chunk(q, carried):
        copy = hop(out_ref, landing, send_sems, recv_sems, q, target)

        @pl.when(here == 0)
        def _():
            x_ref[q] = acts[q]

        @pl.when(here > 0)
        def _():
            copy.wait_recv()
            x_ref[q] = landing[q]

        total = jnp.zeros((rows, tile), F32)
        for r in range(blocks):
            v = x_ref[q, :, columns(r, tile)].astype(F32)
            total = total + v * v
        mean = jnp.sum(total, axis=1, keepdims=True) * (1.0 / (blocks * tile))
        inv_rms = lax.rsqrt(mean + EPSILON)
        for r in range(blocks):
            v = x_ref[q, :, columns(r, tile)].astype(F32)
            hid_ref[q, r] = ((v * inv_rms) * gain[:, columns(r, tile)]).astype(BF16)

        def some_rows(s, unused):
            for i in range(ROWS_PER_STEP):
                r = s * ROWS_PER_STEP + i
                wide = jnp.concatenate([tiles[r * KEEP + j] for j in range(KEEP)], axis=1)
                parts = jnp.dot(hid_ref[q, r], wide, preferred_element_type=F32)
                for j in range(KEEP):
                    parts_ref[r * KEEP + j] = parts[:, j * tile : (j + 1) * tile]
            return unused

        lax.fori_loop(0, blocks // ROWS_PER_STEP, some_rows, 0)

        def some_sums(s, running):
            for i in range(KEEP):
                k = s * KEEP + i
                running = running * keep[k] + parts_ref[order[k]]
                sums_ref[k] = running
            return running

        lax.fori_loop(0, blocks, some_sums, jnp.zeros((rows, tile), F32))
        for r in range(blocks):
            p = sums_ref[last_of[r]] * filled[r]
            pre_ref[q, r] = p
            v = x_ref[q, :, columns(r, tile)].astype(F32)
            out_ref[q, :, columns(r, tile)] = (v + p * sigmoid(p)).astype(BF16)

        @pl.when(here < count - 1)
        def _():
            copy.start()

        return carried

    lax.fori_loop(0, chunks, one_chunk, 0)

    @pl.when(here < count - 1)
    def _():
        for q in range(chunks):
            hop(out_ref, landing, send_sems, recv_sems, q, target).wait_send()


def in_vmem(count):
    return [pl.BlockSpec(memory_space=pltpu.VMEM)] * count


def in_smem(count):
    return [pl.BlockSpec(memory_space=pltpu.SMEM)] * count


def run_forward(tables, acts, gain, gathered):
    chunks, rows, width = acts.shape
    tile_total, tile, _ = gathered.shape
    blocks = width // tile
    cut = (blocks, rows, tile)
    return pl.pallas_call(
        forward_kernel,
        in_specs=in_smem(4) + in_vmem(3),
        out_specs=in_vmem(4),
        out_shape=[
            jax.ShapeDtypeStruct(acts.shape, BF16),
            jax.ShapeDtypeStruct(acts.shape, BF16),
            jax.ShapeDtypeStruct((chunks, *cut), F32),
            jax.ShapeDtypeStruct((chunks, *cut), BF16),
        ],
        scratch_shapes=[
            pltpu.VMEM(acts.shape, BF16),
            pltpu.VMEM((tile_total, rows, tile), F32),
            pltpu.VMEM((tile_total, rows, tile), F32),
            pltpu.SemaphoreType.DMA((chunks,)),
            pltpu.SemaphoreType.DMA((chunks,)),
        ],
        compiler_params=pltpu.CompilerParams(
            vmem_limit_bytes=VMEM_BYTES, collective_id=0, has_side_effects=True
        ),
        cost_estimate=pl.CostEstimate(
            flops=2 * chunks * rows * KEEP * width * tile,
            bytes_accessed=gathered.size * 2,
            transcendentals=chunks * rows * width,
        ),
        name="forward_relay",
    )(*tables, acts, gain, gathered)


def backward_kernel(
    split, cols, lens, cot, gain, tiles, x_in, pre_in,
    grad_ref, pd_ref,
    landing, g_all, gained_ref, dot_ref, send_sems, recv_sems,
):
    chunks, blocks, rows, tile = pre_in.shape
    here, count = lax.axis_index("pipe"), lax.axis_size("pipe")
    target = lax.rem(here + count - 1, count)
    greet()

    def one_chunk(q, carried):
        copy = hop(grad_ref, landing, send_sems, recv_sems, q, target)

        @pl.when(here == count - 1)
        def _():
            start = lax.rem(q, split) * rows
            place = lax.broadcasted_iota(jnp.int32, (rows, tile), 0) + start
            valid = (place < lens[q // split]).astype(F32)
            for r in range(blocks):
                g_all[r] = (cot[q, :, columns(r, tile)].astype(F32) * valid).astype(BF16)

        @pl.when(here < count - 1)
        def _():
            copy.wait_recv()
            for r in range(blocks):
                g_all[r] = landing[q, :, columns(r, tile)]

        total = jnp.zeros((rows, tile), F32)
        for r in range(blocks):
            p = pre_in[q, r]
            s = sigmoid(p)
            g = g_all[r].astype(F32)
            pd_ref[q, r] = (g * s * (1.0 + p * (1.0 - s))).astype(BF16)
            v = x_in[q, :, columns(r, tile)].astype(F32)
            total = total + v * v
        mean = jnp.sum(total, axis=1, keepdims=True) * (1.0 / (blocks * tile))
        inv = jnp.broadcast_to(lax.rsqrt(mean + EPSILON), (rows, tile))
        dot_ref[...] = jnp.zeros_like(dot_ref)

        def some_rows(s, unused):
            for i in range(ROWS_PER_STEP):
                r = s * ROWS_PER_STEP + i
                wide = jnp.concatenate([tiles[r * KEEP + j] for j in range(KEEP)], axis=1)
                picked = jnp.concatenate(
                    [pd_ref[q, cols[r * KEEP + j]] for j in range(KEEP)], axis=1
                )
                delta = lax.dot_general(
                    picked, wide, (((1,), (1,)), ((), ())), preferred_element_type=F32
                )
                at = pl.ds(pl.multiple_of(r * tile, tile), tile)
                gained = delta * gain[:, at]
                gained_ref[r] = gained
                dot_ref[...] += gained * (x_in[q, :, at].astype(F32) * inv)
            return unused

        lax.fori_loop(0, blocks // ROWS_PER_STEP, some_rows, 0)
        mean = jnp.sum(dot_ref[...], axis=1, keepdims=True) * (1.0 / (blocks * tile))
        for r in range(blocks):
            unit = x_in[q, :, columns(r, tile)].astype(F32) * inv
            g = g_all[r].astype(F32) + inv * (gained_ref[r] - unit * mean)
            grad_ref[q, :, columns(r, tile)] = g.astype(BF16)

        @pl.when(here > 0)
        def _():
            copy.start()

        return carried

    lax.fori_loop(0, chunks, one_chunk, 0)

    @pl.when(here > 0)
    def _():
        for q in range(chunks):
            hop(grad_ref, landing, send_sems, recv_sems, q, target).wait_send()


def run_backward(split, cols, lens, cot, gain, gathered, x_all, pre_all):
    chunks, rows, width = cot.shape
    tile = gathered.shape[1]
    cut = (width // tile, rows, tile)
    return pl.pallas_call(
        functools.partial(backward_kernel, split),
        in_specs=in_smem(2) + in_vmem(5),
        out_specs=in_vmem(2),
        out_shape=[
            jax.ShapeDtypeStruct(cot.shape, BF16),
            jax.ShapeDtypeStruct((chunks, *cut), BF16),
        ],
        scratch_shapes=[
            pltpu.VMEM(cot.shape, BF16),
            pltpu.VMEM(cut, BF16),
            pltpu.VMEM(cut, F32),
            pltpu.VMEM((rows, tile), F32),
            pltpu.SemaphoreType.DMA((chunks,)),
            pltpu.SemaphoreType.DMA((chunks,)),
        ],
        compiler_params=pltpu.CompilerParams(
            vmem_limit_bytes=VMEM_BYTES, collective_id=1, has_side_effects=True
        ),
        cost_estimate=pl.CostEstimate(
            flops=2 * chunks * rows * KEEP * width * tile,
            bytes_accessed=gathered.size * 2,
            transcendentals=chunks * rows * width,
        ),
        name="backward_relay",
    )(cols, lens, cot, gain, gathered, x_all, pre_all)


def tile_grad_kernel(per_group, base, cols, hidden, deltas, out_ref):
    share, micros, _, rows, tile = hidden.shape
    start = base[0] + pl.program_id(0) * per_group
    total = None
    for m in range(micros):
        left = hidden[:, m, 0].reshape(share * rows, tile)
        right = jnp.concatenate(
            [
                deltas[:, m, cols[start + j]].reshape(share * rows, tile)
                for j in range(per_group)
            ],
            axis=1,
        )
        term = lax.dot_general(
            left, right, (((0,), (0,)), ((), ())), preferred_element_type=F32
        )
        total = term if total is None else total + term

    @pl.when(pl.program_id(1) == 0)
    def _():
        for j in range(per_group):
            out_ref[j] = total[:, j * tile : (j + 1) * tile]

    @pl.when(pl.program_id(1) > 0)
    def _():
        for j in range(per_group):
            out_ref[j] += total[:, j * tile : (j + 1) * tile]


def run_tile_grad(base, cols, hidden, deltas, tile_count):
    devices, micros, blocks, rows, tile = hidden.shape
    per_group = min(tile_count, KEEP)
    share = min(devices, 8)
    return pl.pallas_call(
        functools.partial(tile_grad_kernel, per_group),
        grid_spec=pltpu.PrefetchScalarGridSpec(
            num_scalar_prefetch=2,
            grid=(tile_count // per_group, devices // share),
            in_specs=[
                pl.BlockSpec(
                    (share, micros, 1, rows, tile),
                    lambda i, k, base, cols: (k, 0, (base[0] + i * per_group) // KEEP, 0, 0),
                )
            ]
            + [
                pl.BlockSpec(
                    (share, micros, blocks, rows, tile),
                    lambda i, k, base, cols: (k, 0, 0, 0, 0),
                )
            ],
            out_specs=pl.BlockSpec(
                (per_group, tile, tile), lambda i, k, base, cols: (i, 0, 0)
            ),
        ),
        out_shape=jax.ShapeDtypeStruct((tile_count, tile, tile), F32),
        compiler_params=pltpu.CompilerParams(vmem_limit_bytes=VMEM_BYTES),
        cost_estimate=pl.CostEstimate(
            flops=2 * tile_count * tile * tile * devices * rows * micros,
            bytes_accessed=2 * devices * micros * blocks * rows * tile,
            transcendentals=0,
        ),
        name="tile_grad",
    )(base, cols, hidden, deltas)


def column_order(cols, blocks):
    spots = jnp.arange(cols.shape[0], dtype=jnp.int32)
    before = jnp.logical_or(
        cols[None, :] < cols[:, None],
        jnp.logical_and(cols[None, :] == cols[:, None], spots[None, :] < spots[:, None]),
    )
    rank = jnp.sum(before.astype(jnp.int32), axis=1)
    hit = (rank[None, :] == spots[:, None]).astype(jnp.int32)
    order = jnp.sum(hit * spots[None, :], axis=1)
    column = jnp.sum(hit * cols[None, :], axis=1)
    same = jnp.concatenate([jnp.zeros((1,), jnp.bool_), column[1:] == column[:-1]])
    blocks_at = jnp.arange(blocks, dtype=jnp.int32)[:, None]
    upto = jnp.sum((cols[None, :] <= blocks_at).astype(jnp.int32), axis=1)
    own = jnp.sum((cols[None, :] == blocks_at).astype(jnp.int32), axis=1)
    return order, same.astype(F32), jnp.maximum(upto - 1, 0), (own > 0).astype(F32)


def on_device(acts_in, cotangent, norm_gains, weights, tile_columns, lengths):
    micros, rows, width = acts_in.shape
    cols = tile_columns[0]
    tile_count, tile = weights.shape[1:3]
    chunks = (micros * SPLIT, rows // SPLIT, width)
    gathered = lax.all_gather(weights[0], "dp", axis=0, tiled=True)
    tables = column_order(cols, width // tile)
    section_out, x_all, pre_all, hid_all = run_forward(
        tables, acts_in.reshape(chunks), norm_gains, gathered
    )
    hidden = lax.all_gather(hid_all, "dp", axis=0)
    input_grad, pd_all = run_backward(
        SPLIT, cols, lengths[:, 0], cotangent.reshape(chunks), norm_gains, gathered, x_all, pre_all
    )
    hidden, pd_all = lax.optimization_barrier((hidden, pd_all))
    deltas = lax.all_gather(pd_all, "dp", axis=0)
    base = (lax.axis_index("dp") * tile_count).astype(jnp.int32).reshape(1)
    weight_grad = run_tile_grad(base, cols, hidden, deltas, tile_count)
    whole = acts_in.shape
    return (section_out.reshape(whole)[None], input_grad.reshape(whole)[None], weight_grad[None])


def solution(mesh):
    return jax.shard_map(
        on_device,
        mesh=mesh,
        in_specs=(
            P(None, "dp", None),
            P(None, "dp", None),
            P("pipe", None),
            P("pipe", "dp", None, None),
            P("pipe", None),
            P(None, "dp"),
        ),
        out_specs=(
            P("pipe", None, "dp", None),
            P("pipe", None, "dp", None),
            P("pipe", "dp", None, None),
        ),
        check_vma=False,
    )
```

```python
import functools

import jax
import jax.numpy as jnp
from jax import lax
from jax.experimental import pallas as pl
from jax.experimental.pallas import tpu as pltpu
from jax.sharding import PartitionSpec as P

KEEP = 8
EPSILON = 1e-05
ROWS_PER_STEP = 4
SPLIT = 2
VMEM_BYTES = 48 * 1024 * 1024

F32 = jnp.float32
BF16 = jnp.bfloat16


def sigmoid(v):
    return 1.0 / (1.0 + jnp.exp(-v))


def columns(block, tile):
    return pl.ds(block * tile, tile)


def greet(sharers=1):
    here, count = lax.axis_index("pipe"), lax.axis_size("pipe")
    barrier = pltpu.get_barrier_semaphore()
    me = lax.axis_index("dp")

    def one_sharer(j, unused):
        pl.semaphore_signal(
            barrier,
            inc=1,
            device_id={"dp": lax.rem(me + j, sharers)},
            device_id_type=pl.DeviceIdType.MESH,
        )
        return unused

    if sharers > 1:
        lax.fori_loop(1, sharers, one_sharer, 0)
    for other in (lax.rem(here + 1, count), lax.rem(here + count - 1, count)):
        pl.semaphore_signal(
            barrier, inc=1, device_id={"pipe": other}, device_id_type=pl.DeviceIdType.MESH
        )
    pl.semaphore_wait(barrier, sharers + 1)


def hop(source, landing, send_sems, recv_sems, chunk, target):
    return pltpu.make_async_remote_copy(
        src_ref=source.at[chunk],
        dst_ref=landing.at[chunk],
        send_sem=send_sems.at[chunk],
        recv_sem=recv_sems.at[chunk],
        device_id={"pipe": target},
        device_id_type=pl.DeviceIdType.MESH,
    )


def to_sharer(source, landing, send_sem, recv_sem, target):
    return pltpu.make_async_remote_copy(
        src_ref=source,
        dst_ref=landing,
        send_sem=send_sem,
        recv_sem=recv_sem,
        device_id={"dp": target},
        device_id_type=pl.DeviceIdType.MESH,
    )


class Exchange:
    def __init__(self, source, landing, out_sems, in_sems, pair_out, pair_in, own_sem):
        self.source, self.landing, self.own_sem = source, landing, own_sem
        self.out_sems, self.in_sems = out_sems, in_sems
        self.pair_out, self.pair_in = pair_out, pair_in
        self.me = lax.axis_index("dp")
        self.chips = lax.axis_size("dp") // 2
        self.chip, self.core = self.me // 2, lax.rem(self.me, 2)
        self.sibling = self.chip * 2 + (1 - self.core)

    def across(self, q, k):
        target = lax.rem(self.chip + k, self.chips) * 2 + self.core
        return to_sharer(
            self.source.at[q], self.landing.at[self.me, q],
            self.out_sems.at[q, k], self.in_sems.at[q, k], target,
        )

    def over(self, q, k):
        owner = lax.rem(self.chip + self.chips - k, self.chips) * 2 + self.core
        piece = self.landing.at[owner, q]
        return to_sharer(
            piece, piece, self.pair_out.at[q, k], self.pair_in.at[q, k], self.sibling
        )

    def own_over(self, q):
        return to_sharer(
            self.source.at[q], self.landing.at[self.me, q],
            self.pair_out.at[q, 0], self.pair_in.at[q, 0], self.sibling,
        )

    def own(self, q):
        return pltpu.make_async_copy(
            self.source.at[q], self.landing.at[self.me, q], self.own_sem.at[q]
        )

    def each(self, act):
        def one(k, unused):
            act(k)
            return unused

        lax.fori_loop(1, self.chips, one, 0)

    def start(self, q):
        self.each(lambda k: self.across(q, k).start())
        self.own_over(q).start()
        self.own(q).start()

    def forward(self, q):
        def act(k):
            self.across(q, k).wait_recv()
            self.over(q, k).start()

        self.each(act)

    def finish(self, q):
        def act(k):
            self.across(q, k).wait_send()
            self.over(q, k).wait()

        self.each(act)
        self.own_over(q).wait()
        self.own(q).wait()


def exchange_sems(pieces, chips):
    return [pltpu.SemaphoreType.DMA((pieces, chips))] * 4 + [pltpu.SemaphoreType.DMA((pieces,))]


def forward_kernel(
    order, keep, last_of, filled, acts, gain, tiles,
    out_ref, x_ref, pre_ref, hid_ref,
    landing, parts_ref, sums_ref, send_sems, recv_sems,
):
    chunks, blocks, rows, tile = pre_ref.shape
    here, count = lax.axis_index("pipe"), lax.axis_size("pipe")
    target = lax.rem(here + 1, count)
    greet()

    def one_chunk(q, carried):
        copy = hop(out_ref, landing, send_sems, recv_sems, q, target)

        @pl.when(here == 0)
        def _():
            x_ref[q] = acts[q]

        @pl.when(here > 0)
        def _():
            copy.wait_recv()
            x_ref[q] = landing[q]

        total = jnp.zeros((rows, tile), F32)
        for r in range(blocks):
            v = x_ref[q, :, columns(r, tile)].astype(F32)
            total = total + v * v
        mean = jnp.sum(total, axis=1, keepdims=True) * (1.0 / (blocks * tile))
        inv_rms = lax.rsqrt(mean + EPSILON)
        for r in range(blocks):
            v = x_ref[q, :, columns(r, tile)].astype(F32)
            hid_ref[q, r] = ((v * inv_rms) * gain[:, columns(r, tile)]).astype(BF16)

        def some_rows(s, unused):
            for i in range(ROWS_PER_STEP):
                r = s * ROWS_PER_STEP + i
                wide = jnp.concatenate([tiles[r * KEEP + j] for j in range(KEEP)], axis=1)
                parts = jnp.dot(hid_ref[q, r], wide, preferred_element_type=F32)
                for j in range(KEEP):
                    parts_ref[r * KEEP + j] = parts[:, j * tile : (j + 1) * tile]
            return unused

        lax.fori_loop(0, blocks // ROWS_PER_STEP, some_rows, 0)

        def some_sums(s, running):
            for i in range(KEEP):
                k = s * KEEP + i
                running = running * keep[k] + parts_ref[order[k]]
                sums_ref[k] = running
            return running

        lax.fori_loop(0, blocks, some_sums, jnp.zeros((rows, tile), F32))
        for r in range(blocks):
            p = sums_ref[last_of[r]] * filled[r]
            pre_ref[q, r] = p
            v = x_ref[q, :, columns(r, tile)].astype(F32)
            out_ref[q, :, columns(r, tile)] = (v + p * sigmoid(p)).astype(BF16)

        @pl.when(here < count - 1)
        def _():
            copy.start()

        return carried

    lax.fori_loop(0, chunks, one_chunk, 0)

    @pl.when(here < count - 1)
    def _():
        for q in range(chunks):
            hop(out_ref, landing, send_sems, recv_sems, q, target).wait_send()


def in_vmem(count):
    return [pl.BlockSpec(memory_space=pltpu.VMEM)] * count


def in_smem(count):
    return [pl.BlockSpec(memory_space=pltpu.SMEM)] * count


def anywhere(count):
    return [pl.BlockSpec(memory_space=pl.ANY)] * count


def run_forward(tables, acts, gain, gathered):
    chunks, rows, width = acts.shape
    tile_total, tile, _ = gathered.shape
    blocks = width // tile
    cut = (blocks, rows, tile)
    return pl.pallas_call(
        forward_kernel,
        in_specs=in_smem(4) + in_vmem(3),
        out_specs=in_vmem(4),
        out_shape=[
            jax.ShapeDtypeStruct(acts.shape, BF16),
            jax.ShapeDtypeStruct(acts.shape, BF16),
            jax.ShapeDtypeStruct((chunks, *cut), F32),
            jax.ShapeDtypeStruct((chunks, *cut), BF16),
        ],
        scratch_shapes=[
            pltpu.VMEM(acts.shape, BF16),
            pltpu.VMEM((tile_total, rows, tile), F32),
            pltpu.VMEM((tile_total, rows, tile), F32),
            pltpu.SemaphoreType.DMA((chunks,)),
            pltpu.SemaphoreType.DMA((chunks,)),
        ],
        compiler_params=pltpu.CompilerParams(
            vmem_limit_bytes=VMEM_BYTES, collective_id=0, has_side_effects=True
        ),
        cost_estimate=pl.CostEstimate(
            flops=2 * chunks * rows * KEEP * width * tile,
            bytes_accessed=gathered.size * 2,
            transcendentals=chunks * rows * width,
        ),
        name="forward_relay",
    )(*tables, acts, gain, gathered)


def backward_kernel(
    split, tile_count, cols, lens, cot, gain, tiles, x_in, pre_in, hid_in,
    grad_ref, deltas_ref, hidden_ref,
    pd_ref, landing, g_all, gained_ref, dot_ref, send_sems, recv_sems,
    hid_out, hid_arrive, hid_own, *sems
):
    chunks, blocks, rows, tile = pre_in.shape
    here, count = lax.axis_index("pipe"), lax.axis_size("pipe")
    target = lax.rem(here + count - 1, count)
    me, sharers = lax.axis_index("dp"), lax.axis_size("dp")
    own_rows = hidden_ref.shape[2]
    deltas = Exchange(pd_ref, deltas_ref, *sems)
    greet(sharers)

    def rows_of(device):
        return hid_in.at[:, pl.ds(device * tile_count // KEEP, own_rows)]

    def hidden_to(j):
        other = lax.rem(me + j, sharers)
        return to_sharer(
            rows_of(other), hidden_ref.at[me], hid_out.at[j], hid_arrive.at[j], other
        )

    def send_hidden(j, unused):
        hidden_to(j).start()
        return unused

    def settle_hidden(j, unused):
        hidden_to(j).wait()
        return unused

    lax.fori_loop(1, sharers, send_hidden, 0)
    hidden_here = pltpu.make_async_copy(rows_of(me), hidden_ref.at[me], hid_own)
    hidden_here.start()

    def one_chunk(q, carried):
        copy = hop(grad_ref, landing, send_sems, recv_sems, q, target)

        @pl.when(here == count - 1)
        def _():
            start = lax.rem(q, split) * rows
            place = lax.broadcasted_iota(jnp.int32, (rows, tile), 0) + start
            valid = (place < lens[q // split]).astype(F32)
            for r in range(blocks):
                g_all[r] = (cot[q, :, columns(r, tile)].astype(F32) * valid).astype(BF16)

        @pl.when(here < count - 1)
        def _():
            copy.wait_recv()
            for r in range(blocks):
                g_all[r] = landing[q, :, columns(r, tile)]

        total = jnp.zeros((rows, tile), F32)
        for r in range(blocks):
            p = pre_in[q, r]
            s = sigmoid(p)
            g = g_all[r].astype(F32)
            pd_ref[q, r] = (g * s * (1.0 + p * (1.0 - s))).astype(BF16)
            v = x_in[q, :, columns(r, tile)].astype(F32)
            total = total + v * v
        deltas.start(q)
        mean = jnp.sum(total, axis=1, keepdims=True) * (1.0 / (blocks * tile))
        inv = jnp.broadcast_to(lax.rsqrt(mean + EPSILON), (rows, tile))
        dot_ref[...] = jnp.zeros_like(dot_ref)

        def some_rows(s, unused):
            for i in range(ROWS_PER_STEP):
                r = s * ROWS_PER_STEP + i
                wide = jnp.concatenate([tiles[r * KEEP + j] for j in range(KEEP)], axis=1)
                picked = jnp.concatenate(
                    [pd_ref[q, cols[r * KEEP + j]] for j in range(KEEP)], axis=1
                )
                delta = lax.dot_general(
                    picked, wide, (((1,), (1,)), ((), ())), preferred_element_type=F32
                )
                at = pl.ds(pl.multiple_of(r * tile, tile), tile)
                gained = delta * gain[:, at]
                gained_ref[r] = gained
                dot_ref[...] += gained * (x_in[q, :, at].astype(F32) * inv)
            return unused

        lax.fori_loop(0, blocks // ROWS_PER_STEP, some_rows, 0)
        mean = jnp.sum(dot_ref[...], axis=1, keepdims=True) * (1.0 / (blocks * tile))
        for r in range(blocks):
            unit = x_in[q, :, columns(r, tile)].astype(F32) * inv
            g = g_all[r].astype(F32) + inv * (gained_ref[r] - unit * mean)
            grad_ref[q, :, columns(r, tile)] = g.astype(BF16)

        @pl.when(here > 0)
        def _():
            copy.start()

        return carried

    lax.fori_loop(0, chunks, one_chunk, 0)

    @pl.when(here > 0)
    def _():
        for q in range(chunks):
            hop(grad_ref, landing, send_sems, recv_sems, q, target).wait_send()

    for act in (deltas.forward, deltas.finish):
        for q in range(chunks):
            act(q)
    lax.fori_loop(1, sharers, settle_hidden, 0)
    hidden_here.wait()


def run_backward(split, tile_count, cols, lens, cot, gain, gathered, x_all, pre_all, hid_all):
    chunks, rows, width = cot.shape
    sharers = lax.axis_size("dp")
    own_rows = max(1, tile_count // KEEP)
    tile = gathered.shape[1]
    cut = (width // tile, rows, tile)
    return pl.pallas_call(
        functools.partial(backward_kernel, split, tile_count),
        in_specs=in_smem(2) + in_vmem(5) + anywhere(1),
        out_specs=in_vmem(1) + anywhere(2),
        out_shape=[
            jax.ShapeDtypeStruct(cot.shape, BF16),
            jax.ShapeDtypeStruct((sharers, chunks, *cut), BF16),
            jax.ShapeDtypeStruct((sharers, chunks, own_rows, rows, tile), BF16),
        ],
        scratch_shapes=[
            pltpu.VMEM((chunks, *cut), BF16),
            pltpu.VMEM(cot.shape, BF16),
            pltpu.VMEM(cut, BF16),
            pltpu.VMEM(cut, F32),
            pltpu.VMEM((rows, tile), F32),
            pltpu.SemaphoreType.DMA((chunks,)),
            pltpu.SemaphoreType.DMA((chunks,)),
            pltpu.SemaphoreType.DMA((sharers,)),
            pltpu.SemaphoreType.DMA((sharers,)),
            pltpu.SemaphoreType.DMA,
        ]
        + exchange_sems(chunks, sharers // 2),
        compiler_params=pltpu.CompilerParams(
            vmem_limit_bytes=VMEM_BYTES, collective_id=1, has_side_effects=True
        ),
        cost_estimate=pl.CostEstimate(
            flops=2 * chunks * rows * KEEP * width * tile,
            bytes_accessed=gathered.size * 2,
            transcendentals=chunks * rows * width,
        ),
        name="backward_relay",
    )(cols, lens, cot, gain, gathered, x_all, pre_all, hid_all)


def tile_grad_kernel(per_group, base, cols, hidden, deltas, out_ref):
    share, micros, _, rows, tile = hidden.shape
    start = base[0] + pl.program_id(0) * per_group
    total = None
    for m in range(micros):
        left = hidden[:, m, 0].reshape(share * rows, tile)
        right = jnp.concatenate(
            [
                deltas[:, m, cols[start + j]].reshape(share * rows, tile)
                for j in range(per_group)
            ],
            axis=1,
        )
        term = lax.dot_general(
            left, right, (((0,), (0,)), ((), ())), preferred_element_type=F32
        )
        total = term if total is None else total + term

    @pl.when(pl.program_id(1) == 0)
    def _():
        for j in range(per_group):
            out_ref[j] = total[:, j * tile : (j + 1) * tile]

    @pl.when(pl.program_id(1) > 0)
    def _():
        for j in range(per_group):
            out_ref[j] += total[:, j * tile : (j + 1) * tile]


def run_tile_grad(base, cols, hidden, deltas, tile_count):
    devices, micros, blocks, rows, tile = deltas.shape
    per_group = min(tile_count, KEEP)
    share = min(devices, 8)
    return pl.pallas_call(
        functools.partial(tile_grad_kernel, per_group),
        grid_spec=pltpu.PrefetchScalarGridSpec(
            num_scalar_prefetch=2,
            grid=(tile_count // per_group, devices // share),
            in_specs=[
                pl.BlockSpec(
                    (share, micros, 1, rows, tile),
                    lambda i, k, base, cols: (
                        k, 0, (base[0] + i * per_group) // KEEP - base[0] // KEEP, 0, 0
                    ),
                )
            ]
            + [
                pl.BlockSpec(
                    (share, micros, blocks, rows, tile),
                    lambda i, k, base, cols: (k, 0, 0, 0, 0),
                )
            ],
            out_specs=pl.BlockSpec(
                (per_group, tile, tile), lambda i, k, base, cols: (i, 0, 0)
            ),
        ),
        out_shape=jax.ShapeDtypeStruct((tile_count, tile, tile), F32),
        compiler_params=pltpu.CompilerParams(vmem_limit_bytes=VMEM_BYTES),
        cost_estimate=pl.CostEstimate(
            flops=2 * tile_count * tile * tile * devices * rows * micros,
            bytes_accessed=2 * devices * micros * blocks * rows * tile,
            transcendentals=0,
        ),
        name="tile_grad",
    )(base, cols, hidden, deltas)


def column_order(cols, blocks):
    spots = jnp.arange(cols.shape[0], dtype=jnp.int32)
    before = jnp.logical_or(
        cols[None, :] < cols[:, None],
        jnp.logical_and(cols[None, :] == cols[:, None], spots[None, :] < spots[:, None]),
    )
    rank = jnp.sum(before.astype(jnp.int32), axis=1)
    hit = (rank[None, :] == spots[:, None]).astype(jnp.int32)
    order = jnp.sum(hit * spots[None, :], axis=1)
    column = jnp.sum(hit * cols[None, :], axis=1)
    same = jnp.concatenate([jnp.zeros((1,), jnp.bool_), column[1:] == column[:-1]])
    blocks_at = jnp.arange(blocks, dtype=jnp.int32)[:, None]
    upto = jnp.sum((cols[None, :] <= blocks_at).astype(jnp.int32), axis=1)
    own = jnp.sum((cols[None, :] == blocks_at).astype(jnp.int32), axis=1)
    return order, same.astype(F32), jnp.maximum(upto - 1, 0), (own > 0).astype(F32)


def on_device(acts_in, cotangent, norm_gains, weights, tile_columns, lengths):
    micros, rows, width = acts_in.shape
    cols = tile_columns[0]
    tile_count, tile = weights.shape[1:3]
    chunks = (micros * SPLIT, rows // SPLIT, width)
    gathered = lax.all_gather(weights[0], "dp", axis=0, tiled=True)
    tables = column_order(cols, width // tile)
    section_out, x_all, pre_all, hid_all = run_forward(
        tables, acts_in.reshape(chunks), norm_gains, gathered
    )
    input_grad, deltas, hidden = run_backward(
        SPLIT, tile_count, cols, lengths[:, 0], cotangent.reshape(chunks), norm_gains, gathered,
        x_all, pre_all, hid_all,
    )
    base = (lax.axis_index("dp") * tile_count).astype(jnp.int32).reshape(1)
    weight_grad = run_tile_grad(base, cols, hidden, deltas, tile_count)
    whole = acts_in.shape
    return (section_out.reshape(whole)[None], input_grad.reshape(whole)[None], weight_grad[None])


def solution(mesh):
    return jax.shard_map(
        on_device,
        mesh=mesh,
        in_specs=(
            P(None, "dp", None),
            P(None, "dp", None),
            P("pipe", None),
            P("pipe", "dp", None, None),
            P("pipe", None),
            P(None, "dp"),
        ),
        out_specs=(
            P("pipe", None, "dp", None),
            P("pipe", None, "dp", None),
            P("pipe", "dp", None, None),
        ),
        check_vma=False,
    )
```

```python
import functools

import jax
import jax.numpy as jnp
from jax import lax
from jax.experimental import pallas as pl
from jax.experimental.pallas import tpu as pltpu
from jax.sharding import PartitionSpec as P

KEEP = 8
EPSILON = 1e-05
ROWS_PER_STEP = 4
SPLIT = 2
PIECES = 4
VMEM_BYTES = 48 * 1024 * 1024

F32 = jnp.float32
BF16 = jnp.bfloat16


def sigmoid(v):
    return 1.0 / (1.0 + jnp.exp(-v))


def columns(block, tile):
    return pl.ds(block * tile, tile)


def greet(sharers=1):
    here, count = lax.axis_index("pipe"), lax.axis_size("pipe")
    barrier = pltpu.get_barrier_semaphore()
    me = lax.axis_index("dp")

    def one_sharer(j, unused):
        pl.semaphore_signal(
            barrier,
            inc=1,
            device_id={"dp": lax.rem(me + j, sharers)},
            device_id_type=pl.DeviceIdType.MESH,
        )
        return unused

    if sharers > 1:
        lax.fori_loop(1, sharers, one_sharer, 0)
    for other in (lax.rem(here + 1, count), lax.rem(here + count - 1, count)):
        pl.semaphore_signal(
            barrier, inc=1, device_id={"pipe": other}, device_id_type=pl.DeviceIdType.MESH
        )
    pl.semaphore_wait(barrier, sharers + 1)


def hop(source, landing, send_sems, recv_sems, chunk, target):
    return pltpu.make_async_remote_copy(
        src_ref=source.at[chunk],
        dst_ref=landing.at[chunk],
        send_sem=send_sems.at[chunk],
        recv_sem=recv_sems.at[chunk],
        device_id={"pipe": target},
        device_id_type=pl.DeviceIdType.MESH,
    )


def to_sharer(source, landing, send_sem, recv_sem, target):
    return pltpu.make_async_remote_copy(
        src_ref=source,
        dst_ref=landing,
        send_sem=send_sem,
        recv_sem=recv_sem,
        device_id={"dp": target},
        device_id_type=pl.DeviceIdType.MESH,
    )


class Exchange:
    def __init__(self, source, landing, out_sems, in_sems, pair_out, pair_in, own_sem):
        self.source, self.landing, self.own_sem = source, landing, own_sem
        self.out_sems, self.in_sems = out_sems, in_sems
        self.pair_out, self.pair_in = pair_out, pair_in
        self.me = lax.axis_index("dp")
        self.chips = lax.axis_size("dp") // 2
        self.chip, self.core = self.me // 2, lax.rem(self.me, 2)
        self.sibling = self.chip * 2 + (1 - self.core)
        self.square = self.chips == 4
        if self.square:
            low, high = lax.rem(self.chip, 2), self.chip // 2
            self.near = {
                1: (high * 2 + 1 - low) * 2 + self.core,
                2: ((1 - high) * 2 + low) * 2 + self.core,
                3: ((1 - high) * 2 + 1 - low) * 2 + self.core,
            }

    def half(self, owner, q, which):
        size = self.landing.shape[2] // 2
        return self.landing.at[owner, q, pl.ds(which * size, size)]

    def across(self, q, k):
        if self.square:
            target = self.near[k]
        else:
            target = lax.rem(self.chip + k, self.chips) * 2 + self.core
        return to_sharer(
            self.source.at[q], self.landing.at[self.me, q],
            self.out_sems.at[q, k], self.in_sems.at[q, k], target,
        )

    def passed_on(self, q, k):
        piece = self.half(self.near[k], q, k - 1)
        return to_sharer(
            piece, piece, self.out_sems.at[q, 2 + k], self.in_sems.at[q, 2 + k], self.near[3 - k]
        )

    def passed_here(self, q, k):
        piece = self.half(self.near[3], q, k - 1)
        return to_sharer(
            piece, piece, self.out_sems.at[q, 2 + k], self.in_sems.at[q, 2 + k], self.near[3 - k]
        )

    def over(self, q, k):
        if self.square and k > 2:
            piece = self.half(self.near[3], q, k - 3)
        elif self.square:
            piece = self.landing.at[self.near[k], q]
        else:
            owner = lax.rem(self.chip + self.chips - k, self.chips) * 2 + self.core
            piece = self.landing.at[owner, q]
        return to_sharer(
            piece, piece, self.pair_out.at[q, k], self.pair_in.at[q, k], self.sibling
        )

    def over_here(self, q, k):
        if self.square:
            flip = 1 - 2 * self.core
            if k > 2:
                piece = self.half(self.near[3] + flip, q, k - 3)
            else:
                piece = self.landing.at[self.near[k] + flip, q]
        else:
            owner = lax.rem(self.chip + self.chips - k, self.chips) * 2 + 1 - self.core
            piece = self.landing.at[owner, q]
        return to_sharer(
            piece, piece, self.pair_out.at[q, k], self.pair_in.at[q, k], self.sibling
        )

    def own_over(self, q):
        return to_sharer(
            self.source.at[q], self.landing.at[self.me, q],
            self.pair_out.at[q, 0], self.pair_in.at[q, 0], self.sibling,
        )

    def own(self, q):
        return pltpu.make_async_copy(
            self.source.at[q], self.landing.at[self.me, q], self.own_sem.at[q]
        )

    def each(self, act):
        def one(k, unused):
            act(k)
            return unused

        if self.square:
            act(1)
            act(2)
        else:
            lax.fori_loop(1, self.chips, one, 0)

    def start(self, q):
        self.each(lambda k: self.across(q, k).start())
        self.own_over(q).start()
        self.own(q).start()

    def forward(self, q):
        def act(k):
            self.across(q, k).wait_recv()
            if self.square:
                self.passed_on(q, k).start()
            self.over(q, k).start()

        self.each(act)

    def last_forward(self, q):
        if self.square:
            for k in (1, 2):
                self.passed_here(q, k).wait_recv()
                self.over(q, 2 + k).start()

    def arrive(self, q):
        self.each(lambda k: self.over_here(q, k).wait_recv())
        if self.square:
            for k in (3, 4):
                self.over_here(q, k).wait_recv()
        self.own_over(q).wait_recv()
        self.own(q).wait()

    def sent(self, q):
        def act(k):
            self.across(q, k).wait_send()
            self.over(q, k).wait_send()

        self.each(act)
        if self.square:
            for k in (1, 2):
                self.passed_on(q, k).wait_send()
                self.over(q, 2 + k).wait_send()
        self.own_over(q).wait_send()


def exchange_sems(pieces, chips):
    width = max(chips, 5)
    return [pltpu.SemaphoreType.DMA((pieces, width))] * 4 + [pltpu.SemaphoreType.DMA((pieces,))]


def forward_kernel(
    order, keep, last_of, filled, acts, gain, share,
    out_ref, x_ref, pre_ref, hid_ref, all_tiles,
    landing, parts_ref, sums_ref, send_sems, recv_sems, *sems
):
    chunks, blocks, rows, tile = pre_ref.shape
    here, count = lax.axis_index("pipe"), lax.axis_size("pipe")
    target = lax.rem(here + 1, count)
    pieces = share.shape[0]
    weights = Exchange(share, all_tiles, *sems)
    tiles = all_tiles.reshape(parts_ref.shape[0], tile, tile)
    greet(lax.axis_size("dp"))
    for act in (weights.start, weights.forward, weights.last_forward, weights.arrive):
        for q in range(pieces):
            act(q)

    def one_chunk(q, carried):
        copy = hop(out_ref, landing, send_sems, recv_sems, q, target)

        @pl.when(here == 0)
        def _():
            x_ref[q] = acts[q]

        @pl.when(here > 0)
        def _():
            copy.wait_recv()
            x_ref[q] = landing[q]

        total = jnp.zeros((rows, tile), F32)
        for r in range(blocks):
            v = x_ref[q, :, columns(r, tile)].astype(F32)
            total = total + v * v
        mean = jnp.sum(total, axis=1, keepdims=True) * (1.0 / (blocks * tile))
        inv_rms = lax.rsqrt(mean + EPSILON)
        for r in range(blocks):
            v = x_ref[q, :, columns(r, tile)].astype(F32)
            hid_ref[q, r] = ((v * inv_rms) * gain[:, columns(r, tile)]).astype(BF16)

        def some_rows(s, unused):
            for i in range(ROWS_PER_STEP):
                r = s * ROWS_PER_STEP + i
                wide = jnp.concatenate([tiles[r * KEEP + j] for j in range(KEEP)], axis=1)
                parts = jnp.dot(hid_ref[q, r], wide, preferred_element_type=F32)
                for j in range(KEEP):
                    parts_ref[r * KEEP + j] = parts[:, j * tile : (j + 1) * tile]
            return unused

        lax.fori_loop(0, blocks // ROWS_PER_STEP, some_rows, 0)

        def some_sums(s, running):
            for i in range(KEEP):
                k = s * KEEP + i
                running = running * keep[k] + parts_ref[order[k]]
                sums_ref[k] = running
            return running

        lax.fori_loop(0, blocks, some_sums, jnp.zeros((rows, tile), F32))
        for r in range(blocks):
            p = sums_ref[last_of[r]] * filled[r]
            pre_ref[q, r] = p
            v = x_ref[q, :, columns(r, tile)].astype(F32)
            out_ref[q, :, columns(r, tile)] = (v + p * sigmoid(p)).astype(BF16)

        @pl.when(here < count - 1)
        def _():
            copy.start()

        return carried

    lax.fori_loop(0, chunks, one_chunk, 0)

    @pl.when(here < count - 1)
    def _():
        for q in range(chunks):
            hop(out_ref, landing, send_sems, recv_sems, q, target).wait_send()

    for q in range(pieces):
        weights.sent(q)


def in_vmem(count):
    return [pl.BlockSpec(memory_space=pltpu.VMEM)] * count


def in_smem(count):
    return [pl.BlockSpec(memory_space=pltpu.SMEM)] * count


def anywhere(count):
    return [pl.BlockSpec(memory_space=pl.ANY)] * count


def run_forward(tables, acts, gain, share):
    chunks, rows, width = acts.shape
    pieces, tile = share.shape[0], share.shape[2]
    sharers = lax.axis_size("dp")
    blocks = width // tile
    tile_total = blocks * KEEP
    cut = (blocks, rows, tile)
    return pl.pallas_call(
        forward_kernel,
        in_specs=in_smem(4) + in_vmem(3),
        out_specs=in_vmem(5),
        out_shape=[
            jax.ShapeDtypeStruct(acts.shape, BF16),
            jax.ShapeDtypeStruct(acts.shape, BF16),
            jax.ShapeDtypeStruct((chunks, *cut), F32),
            jax.ShapeDtypeStruct((chunks, *cut), BF16),
            jax.ShapeDtypeStruct((sharers, *share.shape), BF16),
        ],
        scratch_shapes=[
            pltpu.VMEM(acts.shape, BF16),
            pltpu.VMEM((tile_total, rows, tile), F32),
            pltpu.VMEM((tile_total, rows, tile), F32),
            pltpu.SemaphoreType.DMA((chunks,)),
            pltpu.SemaphoreType.DMA((chunks,)),
        ]
        + exchange_sems(pieces, sharers // 2),
        compiler_params=pltpu.CompilerParams(
            vmem_limit_bytes=VMEM_BYTES, collective_id=0, has_side_effects=True
        ),
        cost_estimate=pl.CostEstimate(
            flops=2 * chunks * rows * KEEP * width * tile,
            bytes_accessed=sharers * share.size * 2,
            transcendentals=chunks * rows * width,
        ),
        name="forward_relay",
    )(*tables, acts, gain, share)


def backward_kernel(
    split, tile_count, cols, lens, cot, gain, tiles, x_in, pre_in, hid_in,
    grad_ref, deltas_ref, hidden_ref,
    pd_ref, landing, g_all, gained_ref, dot_ref, send_sems, recv_sems,
    hid_out, hid_arrive, hid_own, *sems
):
    chunks, blocks, rows, tile = pre_in.shape
    here, count = lax.axis_index("pipe"), lax.axis_size("pipe")
    target = lax.rem(here + count - 1, count)
    me, sharers = lax.axis_index("dp"), lax.axis_size("dp")
    own_rows = hidden_ref.shape[2]
    deltas = Exchange(pd_ref, deltas_ref, *sems)
    greet(sharers)

    def rows_of(device):
        return hid_in.at[:, pl.ds(device * tile_count // KEEP, own_rows)]

    def hidden_to(j):
        other = lax.rem(me + j, sharers)
        return to_sharer(
            rows_of(other), hidden_ref.at[me], hid_out.at[j], hid_arrive.at[j], other
        )

    def send_hidden(j, unused):
        hidden_to(j).start()
        return unused

    def settle_hidden(j, unused):
        hidden_to(j).wait()
        return unused

    lax.fori_loop(1, sharers, send_hidden, 0)
    hidden_here = pltpu.make_async_copy(rows_of(me), hidden_ref.at[me], hid_own)
    hidden_here.start()

    def one_chunk(q, carried):
        copy = hop(grad_ref, landing, send_sems, recv_sems, q, target)

        @pl.when(here == count - 1)
        def _():
            start = lax.rem(q, split) * rows
            place = lax.broadcasted_iota(jnp.int32, (rows, tile), 0) + start
            valid = (place < lens[q // split]).astype(F32)
            for r in range(blocks):
                g_all[r] = (cot[q, :, columns(r, tile)].astype(F32) * valid).astype(BF16)

        @pl.when(here < count - 1)
        def _():
            copy.wait_recv()
            for r in range(blocks):
                g_all[r] = landing[q, :, columns(r, tile)]

        total = jnp.zeros((rows, tile), F32)
        for r in range(blocks):
            p = pre_in[q, r]
            s = sigmoid(p)
            g = g_all[r].astype(F32)
            pd_ref[q, r] = (g * s * (1.0 + p * (1.0 - s))).astype(BF16)
            v = x_in[q, :, columns(r, tile)].astype(F32)
            total = total + v * v
        deltas.start(q)
        mean = jnp.sum(total, axis=1, keepdims=True) * (1.0 / (blocks * tile))
        inv = jnp.broadcast_to(lax.rsqrt(mean + EPSILON), (rows, tile))
        dot_ref[...] = jnp.zeros_like(dot_ref)

        def some_rows(s, unused):
            for i in range(ROWS_PER_STEP):
                r = s * ROWS_PER_STEP + i
                wide = jnp.concatenate([tiles[r * KEEP + j] for j in range(KEEP)], axis=1)
                picked = jnp.concatenate(
                    [pd_ref[q, cols[r * KEEP + j]] for j in range(KEEP)], axis=1
                )
                delta = lax.dot_general(
                    picked, wide, (((1,), (1,)), ((), ())), preferred_element_type=F32
                )
                at = pl.ds(pl.multiple_of(r * tile, tile), tile)
                gained = delta * gain[:, at]
                gained_ref[r] = gained
                dot_ref[...] += gained * (x_in[q, :, at].astype(F32) * inv)
            return unused

        lax.fori_loop(0, blocks // ROWS_PER_STEP, some_rows, 0)
        mean = jnp.sum(dot_ref[...], axis=1, keepdims=True) * (1.0 / (blocks * tile))
        for r in range(blocks):
            unit = x_in[q, :, columns(r, tile)].astype(F32) * inv
            g = g_all[r].astype(F32) + inv * (gained_ref[r] - unit * mean)
            grad_ref[q, :, columns(r, tile)] = g.astype(BF16)

        @pl.when(here > 0)
        def _():
            copy.start()

        @pl.when(jnp.logical_and(here == 0, q > 0))
        def _():
            deltas.forward(q - 1)

        return carried

    lax.fori_loop(0, chunks, one_chunk, 0)

    @pl.when(here > 0)
    def _():
        for q in range(chunks - 1):
            deltas.forward(q)

    deltas.forward(chunks - 1)
    for act in (deltas.last_forward, deltas.arrive, deltas.sent):
        for q in range(chunks):
            act(q)

    @pl.when(here > 0)
    def _():
        for q in range(chunks):
            hop(grad_ref, landing, send_sems, recv_sems, q, target).wait_send()

    lax.fori_loop(1, sharers, settle_hidden, 0)
    hidden_here.wait()


def run_backward(split, tile_count, cols, lens, cot, gain, gathered, x_all, pre_all, hid_all):
    chunks, rows, width = cot.shape
    sharers = lax.axis_size("dp")
    own_rows = max(1, tile_count // KEEP)
    tile = gathered.shape[1]
    cut = (width // tile, rows, tile)
    return pl.pallas_call(
        functools.partial(backward_kernel, split, tile_count),
        in_specs=in_smem(2) + in_vmem(5) + anywhere(1),
        out_specs=in_vmem(1) + anywhere(2),
        out_shape=[
            jax.ShapeDtypeStruct(cot.shape, BF16),
            jax.ShapeDtypeStruct((sharers, chunks, *cut), BF16),
            jax.ShapeDtypeStruct((sharers, chunks, own_rows, rows, tile), BF16),
        ],
        scratch_shapes=[
            pltpu.VMEM((chunks, *cut), BF16),
            pltpu.VMEM(cot.shape, BF16),
            pltpu.VMEM(cut, BF16),
            pltpu.VMEM(cut, F32),
            pltpu.VMEM((rows, tile), F32),
            pltpu.SemaphoreType.DMA((chunks,)),
            pltpu.SemaphoreType.DMA((chunks,)),
            pltpu.SemaphoreType.DMA((sharers,)),
            pltpu.SemaphoreType.DMA((sharers,)),
            pltpu.SemaphoreType.DMA,
        ]
        + exchange_sems(chunks, sharers // 2),
        compiler_params=pltpu.CompilerParams(
            vmem_limit_bytes=VMEM_BYTES, collective_id=1, has_side_effects=True
        ),
        cost_estimate=pl.CostEstimate(
            flops=2 * chunks * rows * KEEP * width * tile,
            bytes_accessed=gathered.size * 2,
            transcendentals=chunks * rows * width,
        ),
        name="backward_relay",
    )(cols, lens, cot, gain, gathered, x_all, pre_all, hid_all)


def tile_grad_kernel(per_group, base, cols, hidden, deltas, out_ref):
    share, micros, _, rows, tile = hidden.shape
    start = base[0] + pl.program_id(0) * per_group
    total = None
    for m in range(micros):
        left = hidden[:, m, 0].reshape(share * rows, tile)
        right = jnp.concatenate(
            [
                deltas[:, m, cols[start + j]].reshape(share * rows, tile)
                for j in range(per_group)
            ],
            axis=1,
        )
        term = lax.dot_general(
            left, right, (((0,), (0,)), ((), ())), preferred_element_type=F32
        )
        total = term if total is None else total + term

    @pl.when(pl.program_id(1) == 0)
    def _():
        for j in range(per_group):
            out_ref[j] = total[:, j * tile : (j + 1) * tile]

    @pl.when(pl.program_id(1) > 0)
    def _():
        for j in range(per_group):
            out_ref[j] += total[:, j * tile : (j + 1) * tile]


def run_tile_grad(base, cols, hidden, deltas, tile_count):
    devices, micros, blocks, rows, tile = deltas.shape
    per_group = min(tile_count, KEEP)
    share = min(devices, 8)
    return pl.pallas_call(
        functools.partial(tile_grad_kernel, per_group),
        grid_spec=pltpu.PrefetchScalarGridSpec(
            num_scalar_prefetch=2,
            grid=(tile_count // per_group, devices // share),
            in_specs=[
                pl.BlockSpec(
                    (share, micros, 1, rows, tile),
                    lambda i, k, base, cols: (
                        k, 0, (base[0] + i * per_group) // KEEP - base[0] // KEEP, 0, 0
                    ),
                )
            ]
            + [
                pl.BlockSpec(
                    (share, micros, blocks, rows, tile),
                    lambda i, k, base, cols: (k, 0, 0, 0, 0),
                )
            ],
            out_specs=pl.BlockSpec(
                (per_group, tile, tile), lambda i, k, base, cols: (i, 0, 0)
            ),
        ),
        out_shape=jax.ShapeDtypeStruct((tile_count, tile, tile), F32),
        compiler_params=pltpu.CompilerParams(vmem_limit_bytes=VMEM_BYTES),
        cost_estimate=pl.CostEstimate(
            flops=2 * tile_count * tile * tile * devices * rows * micros,
            bytes_accessed=2 * devices * micros * blocks * rows * tile,
            transcendentals=0,
        ),
        name="tile_grad",
    )(base, cols, hidden, deltas)


def column_order(cols, blocks):
    spots = jnp.arange(cols.shape[0], dtype=jnp.int32)
    before = jnp.logical_or(
        cols[None, :] < cols[:, None],
        jnp.logical_and(cols[None, :] == cols[:, None], spots[None, :] < spots[:, None]),
    )
    rank = jnp.sum(before.astype(jnp.int32), axis=1)
    hit = (rank[None, :] == spots[:, None]).astype(jnp.int32)
    order = jnp.sum(hit * spots[None, :], axis=1)
    column = jnp.sum(hit * cols[None, :], axis=1)
    same = jnp.concatenate([jnp.zeros((1,), jnp.bool_), column[1:] == column[:-1]])
    blocks_at = jnp.arange(blocks, dtype=jnp.int32)[:, None]
    upto = jnp.sum((cols[None, :] <= blocks_at).astype(jnp.int32), axis=1)
    own = jnp.sum((cols[None, :] == blocks_at).astype(jnp.int32), axis=1)
    return order, same.astype(F32), jnp.maximum(upto - 1, 0), (own > 0).astype(F32)


def on_device(acts_in, cotangent, norm_gains, weights, tile_columns, lengths):
    micros, rows, width = acts_in.shape
    cols = tile_columns[0]
    tile_count, tile = weights.shape[1:3]
    chunks = (micros * SPLIT, rows // SPLIT, width)
    share = weights[0].reshape(PIECES, tile_count // PIECES, tile, tile)
    tables = column_order(cols, width // tile)
    section_out, x_all, pre_all, hid_all, gathered = run_forward(
        tables, acts_in.reshape(chunks), norm_gains, share
    )
    gathered = gathered.reshape(-1, tile, tile)
    input_grad, deltas, hidden = run_backward(
        SPLIT, tile_count, cols, lengths[:, 0], cotangent.reshape(chunks), norm_gains, gathered,
        x_all, pre_all, hid_all,
    )
    base = (lax.axis_index("dp") * tile_count).astype(jnp.int32).reshape(1)
    weight_grad = run_tile_grad(base, cols, hidden, deltas, tile_count)
    whole = acts_in.shape
    return (section_out.reshape(whole)[None], input_grad.reshape(whole)[None], weight_grad[None])


def solution(mesh):
    return jax.shard_map(
        on_device,
        mesh=mesh,
        in_specs=(
            P(None, "dp", None),
            P(None, "dp", None),
            P("pipe", None),
            P("pipe", "dp", None, None),
            P("pipe", None),
            P(None, "dp"),
        ),
        out_specs=(
            P("pipe", None, "dp", None),
            P("pipe", None, "dp", None),
            P("pipe", "dp", None, None),
        ),
        check_vma=False,
    )
```

```python
import functools

import jax
import jax.numpy as jnp
from jax import lax
from jax.experimental import pallas as pl
from jax.experimental.pallas import tpu as pltpu
from jax.sharding import PartitionSpec as P

KEEP = 8
EPSILON = 1e-05
ROWS_PER_STEP = 4
SPLIT = 2
PIECES = 8
VMEM_BYTES = 48 * 1024 * 1024

F32 = jnp.float32
BF16 = jnp.bfloat16


def sigmoid(v):
    return 1.0 / (1.0 + jnp.exp(-v))


def columns(block, tile):
    return pl.ds(block * tile, tile)


def greet(sharers=1):
    here, count = lax.axis_index("pipe"), lax.axis_size("pipe")
    barrier = pltpu.get_barrier_semaphore()
    me = lax.axis_index("dp")

    def one_sharer(j, unused):
        pl.semaphore_signal(
            barrier,
            inc=1,
            device_id={"dp": lax.rem(me + j, sharers)},
            device_id_type=pl.DeviceIdType.MESH,
        )
        return unused

    if sharers > 1:
        lax.fori_loop(1, sharers, one_sharer, 0)
    for other in (lax.rem(here + 1, count), lax.rem(here + count - 1, count)):
        pl.semaphore_signal(
            barrier, inc=1, device_id={"pipe": other}, device_id_type=pl.DeviceIdType.MESH
        )
    pl.semaphore_wait(barrier, sharers + 1)


def hop(source, landing, send_sems, recv_sems, chunk, target):
    return pltpu.make_async_remote_copy(
        src_ref=source.at[chunk],
        dst_ref=landing.at[chunk],
        send_sem=send_sems.at[chunk],
        recv_sem=recv_sems.at[chunk],
        device_id={"pipe": target},
        device_id_type=pl.DeviceIdType.MESH,
    )


def to_sharer(source, landing, send_sem, recv_sem, target):
    return pltpu.make_async_remote_copy(
        src_ref=source,
        dst_ref=landing,
        send_sem=send_sem,
        recv_sem=recv_sem,
        device_id={"dp": target},
        device_id_type=pl.DeviceIdType.MESH,
    )


class Exchange:
    def __init__(self, source, landing, out_sems, in_sems, pair_out, pair_in, own_sem):
        self.source, self.landing, self.own_sem = source, landing, own_sem
        self.out_sems, self.in_sems = out_sems, in_sems
        self.pair_out, self.pair_in = pair_out, pair_in
        self.me = lax.axis_index("dp")
        self.chips = lax.axis_size("dp") // 2
        self.chip, self.core = self.me // 2, lax.rem(self.me, 2)
        self.sibling = self.chip * 2 + (1 - self.core)
        self.square = self.chips == 4
        if self.square:
            low, high = lax.rem(self.chip, 2), self.chip // 2
            self.near = {
                1: (high * 2 + 1 - low) * 2 + self.core,
                2: ((1 - high) * 2 + low) * 2 + self.core,
                3: ((1 - high) * 2 + 1 - low) * 2 + self.core,
            }

    def half(self, owner, q, which):
        size = self.landing.shape[2] // 2
        return self.landing.at[owner, q, pl.ds(which * size, size)]

    def across(self, q, k):
        if self.square:
            target = self.near[k]
        else:
            target = lax.rem(self.chip + k, self.chips) * 2 + self.core
        return to_sharer(
            self.source.at[q], self.landing.at[self.me, q],
            self.out_sems.at[q, k], self.in_sems.at[q, k], target,
        )

    def passed_on(self, q, k):
        piece = self.half(self.near[k], q, k - 1)
        return to_sharer(
            piece, piece, self.out_sems.at[q, 2 + k], self.in_sems.at[q, 2 + k], self.near[3 - k]
        )

    def passed_here(self, q, k):
        piece = self.half(self.near[3], q, k - 1)
        return to_sharer(
            piece, piece, self.out_sems.at[q, 2 + k], self.in_sems.at[q, 2 + k], self.near[3 - k]
        )

    def over(self, q, k):
        if self.square and k > 2:
            piece = self.half(self.near[3], q, k - 3)
        elif self.square:
            piece = self.landing.at[self.near[k], q]
        else:
            owner = lax.rem(self.chip + self.chips - k, self.chips) * 2 + self.core
            piece = self.landing.at[owner, q]
        return to_sharer(
            piece, piece, self.pair_out.at[q, k], self.pair_in.at[q, k], self.sibling
        )

    def over_here(self, q, k):
        if self.square:
            flip = 1 - 2 * self.core
            if k > 2:
                piece = self.half(self.near[3] + flip, q, k - 3)
            else:
                piece = self.landing.at[self.near[k] + flip, q]
        else:
            owner = lax.rem(self.chip + self.chips - k, self.chips) * 2 + 1 - self.core
            piece = self.landing.at[owner, q]
        return to_sharer(
            piece, piece, self.pair_out.at[q, k], self.pair_in.at[q, k], self.sibling
        )

    def own_over(self, q):
        return to_sharer(
            self.source.at[q], self.landing.at[self.me, q],
            self.pair_out.at[q, 0], self.pair_in.at[q, 0], self.sibling,
        )

    def own(self, q):
        return pltpu.make_async_copy(
            self.source.at[q], self.landing.at[self.me, q], self.own_sem.at[q]
        )

    def each(self, act):
        def one(k, unused):
            act(k)
            return unused

        if self.square:
            act(1)
            act(2)
        else:
            lax.fori_loop(1, self.chips, one, 0)

    def start(self, q):
        self.each(lambda k: self.across(q, k).start())
        self.own_over(q).start()
        self.own(q).start()

    def forward(self, q):
        def act(k):
            self.across(q, k).wait_recv()
            if self.square:
                self.passed_on(q, k).start()
            self.over(q, k).start()

        self.each(act)

    def last_forward(self, q):
        if self.square:
            for k in (1, 2):
                self.passed_here(q, k).wait_recv()
                self.over(q, 2 + k).start()

    def arrive(self, q):
        self.each(lambda k: self.over_here(q, k).wait_recv())
        if self.square:
            for k in (3, 4):
                self.over_here(q, k).wait_recv()
        self.own_over(q).wait_recv()
        self.own(q).wait()

    def sent(self, q):
        def act(k):
            self.across(q, k).wait_send()
            self.over(q, k).wait_send()

        self.each(act)
        if self.square:
            for k in (1, 2):
                self.passed_on(q, k).wait_send()
                self.over(q, 2 + k).wait_send()
        self.own_over(q).wait_send()


def exchange_sems(pieces, chips):
    width = max(chips, 5)
    return [pltpu.SemaphoreType.DMA((pieces, width))] * 4 + [pltpu.SemaphoreType.DMA((pieces,))]


def forward_kernel(
    order, keep, last_of, filled, acts, gain, share,
    out_ref, x_ref, pre_ref, hid_ref, all_tiles,
    landing, parts_ref, sums_ref, send_sems, recv_sems, first_sem, *sems
):
    chunks, blocks, rows, tile = pre_ref.shape
    here, count = lax.axis_index("pipe"), lax.axis_size("pipe")
    target = lax.rem(here + 1, count)
    pieces = share.shape[0]
    weights = Exchange(share, all_tiles, *sems)
    tiles = all_tiles.reshape(parts_ref.shape[0], tile, tile)
    greet(lax.axis_size("dp"))
    first = pltpu.make_async_copy(acts, landing, first_sem)

    @pl.when(here == 0)
    def _():
        first.start()

    for act in (weights.start, weights.forward, weights.last_forward, weights.arrive):
        for q in range(pieces):
            act(q)

    @pl.when(here == 0)
    def _():
        first.wait()

    def one_chunk(q, carried):
        copy = hop(out_ref, landing, send_sems, recv_sems, q, target)

        @pl.when(here > 0)
        def _():
            copy.wait_recv()

        x_ref[q] = landing[q]
        total = jnp.zeros((rows, tile), F32)
        for r in range(blocks):
            v = x_ref[q, :, columns(r, tile)].astype(F32)
            total = total + v * v
        mean = jnp.sum(total, axis=1, keepdims=True) * (1.0 / (blocks * tile))
        inv_rms = lax.rsqrt(mean + EPSILON)
        for r in range(blocks):
            v = x_ref[q, :, columns(r, tile)].astype(F32)
            hid_ref[q, r] = ((v * inv_rms) * gain[:, columns(r, tile)]).astype(BF16)

        def some_rows(s, unused):
            for i in range(ROWS_PER_STEP):
                r = s * ROWS_PER_STEP + i
                wide = jnp.concatenate([tiles[r * KEEP + j] for j in range(KEEP)], axis=1)
                parts = jnp.dot(hid_ref[q, r], wide, preferred_element_type=F32)
                for j in range(KEEP):
                    parts_ref[r * KEEP + j] = parts[:, j * tile : (j + 1) * tile]
            return unused

        lax.fori_loop(0, blocks // ROWS_PER_STEP, some_rows, 0)

        def some_sums(s, running):
            for i in range(KEEP):
                k = s * KEEP + i
                running = running * keep[k] + parts_ref[order[k]]
                sums_ref[k] = running
            return running

        lax.fori_loop(0, blocks, some_sums, jnp.zeros((rows, tile), F32))
        for r in range(blocks):
            p = sums_ref[last_of[r]] * filled[r]
            pre_ref[q, r] = p
            v = x_ref[q, :, columns(r, tile)].astype(F32)
            out_ref[q, :, columns(r, tile)] = (v + p * sigmoid(p)).astype(BF16)

        @pl.when(here < count - 1)
        def _():
            copy.start()

        return carried

    lax.fori_loop(0, chunks, one_chunk, 0)

    @pl.when(here < count - 1)
    def _():
        for q in range(chunks):
            hop(out_ref, landing, send_sems, recv_sems, q, target).wait_send()

    for q in range(pieces):
        weights.sent(q)


def in_vmem(count):
    return [pl.BlockSpec(memory_space=pltpu.VMEM)] * count


def in_smem(count):
    return [pl.BlockSpec(memory_space=pltpu.SMEM)] * count


def anywhere(count):
    return [pl.BlockSpec(memory_space=pl.ANY)] * count


def run_forward(tables, acts, gain, share):
    chunks, rows, width = acts.shape
    pieces, tile = share.shape[0], share.shape[2]
    sharers = lax.axis_size("dp")
    blocks = width // tile
    tile_total = blocks * KEEP
    cut = (blocks, rows, tile)
    return pl.pallas_call(
        forward_kernel,
        in_specs=in_smem(4) + anywhere(1) + in_vmem(1) + anywhere(1),
        out_specs=in_vmem(5),
        out_shape=[
            jax.ShapeDtypeStruct(acts.shape, BF16),
            jax.ShapeDtypeStruct(acts.shape, BF16),
            jax.ShapeDtypeStruct((chunks, *cut), F32),
            jax.ShapeDtypeStruct((chunks, *cut), BF16),
            jax.ShapeDtypeStruct((sharers, *share.shape), BF16),
        ],
        scratch_shapes=[
            pltpu.VMEM(acts.shape, BF16),
            pltpu.VMEM((tile_total, rows, tile), F32),
            pltpu.VMEM((tile_total, rows, tile), F32),
            pltpu.SemaphoreType.DMA((chunks,)),
            pltpu.SemaphoreType.DMA((chunks,)),
            pltpu.SemaphoreType.DMA,
        ]
        + exchange_sems(pieces, sharers // 2),
        compiler_params=pltpu.CompilerParams(
            vmem_limit_bytes=VMEM_BYTES, collective_id=0, has_side_effects=True
        ),
        cost_estimate=pl.CostEstimate(
            flops=2 * chunks * rows * KEEP * width * tile,
            bytes_accessed=sharers * share.size * 2,
            transcendentals=chunks * rows * width,
        ),
        name="forward_relay",
    )(*tables, acts, gain, share)


def backward_kernel(
    split, tile_count, cols, lens, cot, gain, tiles, x_in, pre_in, hid_in,
    grad_ref, deltas_ref, hidden_ref,
    pd_ref, landing, g_all, gained_ref, dot_ref, send_sems, recv_sems,
    hid_out, hid_arrive, hid_own, first_sem, *sems
):
    chunks, blocks, rows, tile = pre_in.shape
    here, count = lax.axis_index("pipe"), lax.axis_size("pipe")
    target = lax.rem(here + count - 1, count)
    me, sharers = lax.axis_index("dp"), lax.axis_size("dp")
    own_rows = hidden_ref.shape[2]
    deltas = Exchange(pd_ref, deltas_ref, *sems)
    first = pltpu.make_async_copy(cot, landing, first_sem)

    @pl.when(here == count - 1)
    def _():
        first.start()

    greet(sharers)

    def rows_of(device):
        return hid_in.at[:, pl.ds(device * tile_count // KEEP, own_rows)]

    def hidden_to(j):
        other = lax.rem(me + j, sharers)
        return to_sharer(
            rows_of(other), hidden_ref.at[me], hid_out.at[j], hid_arrive.at[j], other
        )

    def send_hidden(j, unused):
        hidden_to(j).start()
        return unused

    def settle_hidden(j, unused):
        hidden_to(j).wait()
        return unused

    lax.fori_loop(1, sharers, send_hidden, 0)
    hidden_here = pltpu.make_async_copy(rows_of(me), hidden_ref.at[me], hid_own)
    hidden_here.start()

    @pl.when(here == count - 1)
    def _():
        first.wait()


    def one_chunk(q, carried):
        copy = hop(grad_ref, landing, send_sems, recv_sems, q, target)

        @pl.when(here == count - 1)
        def _():
            start = lax.rem(q, split) * rows
            place = lax.broadcasted_iota(jnp.int32, (rows, tile), 0) + start
            valid = (place < lens[q // split]).astype(F32)
            for r in range(blocks):
                g_all[r] = (landing[q, :, columns(r, tile)].astype(F32) * valid).astype(BF16)

        @pl.when(here < count - 1)
        def _():
            copy.wait_recv()
            for r in range(blocks):
                g_all[r] = landing[q, :, columns(r, tile)]

        total = jnp.zeros((rows, tile), F32)
        for r in range(blocks):
            p = pre_in[q, r]
            s = sigmoid(p)
            g = g_all[r].astype(F32)
            pd_ref[q, r] = (g * s * (1.0 + p * (1.0 - s))).astype(BF16)
            v = x_in[q, :, columns(r, tile)].astype(F32)
            total = total + v * v
        deltas.start(q)
        mean = jnp.sum(total, axis=1, keepdims=True) * (1.0 / (blocks * tile))
        inv = jnp.broadcast_to(lax.rsqrt(mean + EPSILON), (rows, tile))
        dot_ref[...] = jnp.zeros_like(dot_ref)

        def some_rows(s, unused):
            for i in range(ROWS_PER_STEP):
                r = s * ROWS_PER_STEP + i
                wide = jnp.concatenate([tiles[r * KEEP + j] for j in range(KEEP)], axis=1)
                picked = jnp.concatenate(
                    [pd_ref[q, cols[r * KEEP + j]] for j in range(KEEP)], axis=1
                )
                delta = lax.dot_general(
                    picked, wide, (((1,), (1,)), ((), ())), preferred_element_type=F32
                )
                at = pl.ds(pl.multiple_of(r * tile, tile), tile)
                gained = delta * gain[:, at]
                gained_ref[r] = gained
                dot_ref[...] += gained * (x_in[q, :, at].astype(F32) * inv)
            return unused

        lax.fori_loop(0, blocks // ROWS_PER_STEP, some_rows, 0)
        mean = jnp.sum(dot_ref[...], axis=1, keepdims=True) * (1.0 / (blocks * tile))
        for r in range(blocks):
            unit = x_in[q, :, columns(r, tile)].astype(F32) * inv
            g = g_all[r].astype(F32) + inv * (gained_ref[r] - unit * mean)
            grad_ref[q, :, columns(r, tile)] = g.astype(BF16)

        @pl.when(here > 0)
        def _():
            copy.start()

        @pl.when(jnp.logical_and(here == 0, q > 0))
        def _():
            deltas.forward(q - 1)

        return carried

    lax.fori_loop(0, chunks, one_chunk, 0)

    @pl.when(here > 0)
    def _():
        for q in range(chunks - 1):
            deltas.forward(q)

    deltas.forward(chunks - 1)
    for act in (deltas.last_forward, deltas.arrive, deltas.sent):
        for q in range(chunks):
            act(q)

    @pl.when(here > 0)
    def _():
        for q in range(chunks):
            hop(grad_ref, landing, send_sems, recv_sems, q, target).wait_send()

    lax.fori_loop(1, sharers, settle_hidden, 0)
    hidden_here.wait()


def run_backward(split, tile_count, cols, lens, cot, gain, gathered, x_all, pre_all, hid_all):
    chunks, rows, width = cot.shape
    sharers = lax.axis_size("dp")
    own_rows = max(1, tile_count // KEEP)
    tile = gathered.shape[1]
    cut = (width // tile, rows, tile)
    return pl.pallas_call(
        functools.partial(backward_kernel, split, tile_count),
        in_specs=in_smem(2) + anywhere(1) + in_vmem(4) + anywhere(1),
        out_specs=in_vmem(1) + anywhere(2),
        out_shape=[
            jax.ShapeDtypeStruct(cot.shape, BF16),
            jax.ShapeDtypeStruct((sharers, chunks, *cut), BF16),
            jax.ShapeDtypeStruct((sharers, chunks, own_rows, rows, tile), BF16),
        ],
        scratch_shapes=[
            pltpu.VMEM((chunks, *cut), BF16),
            pltpu.VMEM(cot.shape, BF16),
            pltpu.VMEM(cut, BF16),
            pltpu.VMEM(cut, F32),
            pltpu.VMEM((rows, tile), F32),
            pltpu.SemaphoreType.DMA((chunks,)),
            pltpu.SemaphoreType.DMA((chunks,)),
            pltpu.SemaphoreType.DMA((sharers,)),
            pltpu.SemaphoreType.DMA((sharers,)),
            pltpu.SemaphoreType.DMA,
            pltpu.SemaphoreType.DMA,
        ]
        + exchange_sems(chunks, sharers // 2),
        compiler_params=pltpu.CompilerParams(
            vmem_limit_bytes=VMEM_BYTES, collective_id=1, has_side_effects=True
        ),
        cost_estimate=pl.CostEstimate(
            flops=2 * chunks * rows * KEEP * width * tile,
            bytes_accessed=gathered.size * 2,
            transcendentals=chunks * rows * width,
        ),
        name="backward_relay",
    )(cols, lens, cot, gain, gathered, x_all, pre_all, hid_all)


def tile_grad_kernel(per_group, base, cols, hidden, deltas, out_ref):
    share, micros, _, rows, tile = hidden.shape
    group = pl.program_id(1)
    start = base[0] + group * per_group
    depth = share * micros * rows
    right = jnp.concatenate(
        [deltas[:, :, cols[start + j]].reshape(depth, tile) for j in range(per_group)], axis=1
    )
    total = lax.dot_general(
        hidden[:, :, 0].reshape(depth, tile), right, (((0,), (0,)), ((), ())),
        preferred_element_type=F32,
    )

    @pl.when(pl.program_id(0) == 0)
    def _():
        for j in range(per_group):
            out_ref[group * per_group + j] = total[:, j * tile : (j + 1) * tile]

    @pl.when(pl.program_id(0) > 0)
    def _():
        for j in range(per_group):
            out_ref[group * per_group + j] += total[:, j * tile : (j + 1) * tile]


def run_tile_grad(base, cols, hidden, deltas, tile_count):
    devices, micros, blocks, rows, tile = deltas.shape
    per_group = min(tile_count, KEEP)
    share = min(devices, 2)
    return pl.pallas_call(
        functools.partial(tile_grad_kernel, per_group),
        grid_spec=pltpu.PrefetchScalarGridSpec(
            num_scalar_prefetch=2,
            grid=(devices // share, tile_count // per_group),
            in_specs=[
                pl.BlockSpec(
                    (share, micros, 1, rows, tile),
                    lambda k, i, base, cols: (
                        k, 0, (base[0] + i * per_group) // KEEP - base[0] // KEEP, 0, 0
                    ),
                )
            ]
            + [
                pl.BlockSpec(
                    (share, micros, blocks, rows, tile),
                    lambda k, i, base, cols: (k, 0, 0, 0, 0),
                )
            ],
            out_specs=pl.BlockSpec(
                (tile_count, tile, tile), lambda k, i, base, cols: (0, 0, 0)
            ),
        ),
        out_shape=jax.ShapeDtypeStruct((tile_count, tile, tile), F32),
        compiler_params=pltpu.CompilerParams(vmem_limit_bytes=VMEM_BYTES),
        cost_estimate=pl.CostEstimate(
            flops=2 * tile_count * tile * tile * devices * rows * micros,
            bytes_accessed=2 * devices * micros * blocks * rows * tile,
            transcendentals=0,
        ),
        name="tile_grad",
    )(base, cols, hidden, deltas)


def column_order(cols, blocks):
    spots = jnp.arange(cols.shape[0], dtype=jnp.int32)
    before = jnp.logical_or(
        cols[None, :] < cols[:, None],
        jnp.logical_and(cols[None, :] == cols[:, None], spots[None, :] < spots[:, None]),
    )
    rank = jnp.sum(before.astype(jnp.int32), axis=1)
    hit = (rank[None, :] == spots[:, None]).astype(jnp.int32)
    order = jnp.sum(hit * spots[None, :], axis=1)
    column = jnp.sum(hit * cols[None, :], axis=1)
    same = jnp.concatenate([jnp.zeros((1,), jnp.bool_), column[1:] == column[:-1]])
    blocks_at = jnp.arange(blocks, dtype=jnp.int32)[:, None]
    upto = jnp.sum((cols[None, :] <= blocks_at).astype(jnp.int32), axis=1)
    own = jnp.sum((cols[None, :] == blocks_at).astype(jnp.int32), axis=1)
    return order, same.astype(F32), jnp.maximum(upto - 1, 0), (own > 0).astype(F32)


def on_device(acts_in, cotangent, norm_gains, weights, tile_columns, lengths):
    micros, rows, width = acts_in.shape
    cols = tile_columns[0]
    tile_count, tile = weights.shape[1:3]
    chunks = (micros * SPLIT, rows // SPLIT, width)
    pieces = min(PIECES, tile_count)
    share = weights[0].reshape(pieces, tile_count // pieces, tile, tile)
    tables = column_order(cols, width // tile)
    section_out, x_all, pre_all, hid_all, gathered = run_forward(
        tables, acts_in.reshape(chunks), norm_gains, share
    )
    gathered = gathered.reshape(-1, tile, tile)
    input_grad, deltas, hidden = run_backward(
        SPLIT, tile_count, cols, lengths[:, 0], cotangent.reshape(chunks), norm_gains, gathered,
        x_all, pre_all, hid_all,
    )
    base = (lax.axis_index("dp") * tile_count).astype(jnp.int32).reshape(1)
    weight_grad = run_tile_grad(base, cols, hidden, deltas, tile_count)
    whole = acts_in.shape
    return (section_out.reshape(whole)[None], input_grad.reshape(whole)[None], weight_grad[None])


def solution(mesh):
    return jax.shard_map(
        on_device,
        mesh=mesh,
        in_specs=(
            P(None, "dp", None),
            P(None, "dp", None),
            P("pipe", None),
            P("pipe", "dp", None, None),
            P("pipe", None),
            P(None, "dp"),
        ),
        out_specs=(
            P("pipe", None, "dp", None),
            P("pipe", None, "dp", None),
            P("pipe", "dp", None, None),
        ),
        check_vma=False,
    )
```
